32 devices in a mesh: dp: 4 (over x, core), blk: 4 (over z), fsdp: 2 (over y).
Axes of the slice: x: 2, y: 2, z: 4, core: 2. Of those that a mesh axis runs over, the one named last changes fastest.
Arguments:
- hidden_in: bfloat16 [8, 1024, 2048], P('dp', ('blk', 'fsdp')), may hold values from -6 to 6
- out_grad: bfloat16 [8, 1024, 2048], P('dp', ('blk', 'fsdp')), may hold values from -6 to 6
- doc_lengths: int32 [8, 4], P('dp'), may hold values from 1 to 960, as said below
- norm_attn: bfloat16 [2048], P(('dp', 'blk', 'fsdp')), may hold values from 0.5 to 1.5
- query_gain: bfloat16 [128], P(('dp', 'blk', 'fsdp')), may hold values from 0.5 to 1.5
- key_gain: bfloat16 [128], P(('dp', 'blk', 'fsdp')), may hold values from 0.5 to 1.5
- query_weight: bfloat16 [2048, 2048], P(('dp', 'blk', 'fsdp')), may hold values from -0.125 to 0.125
- key_weight: bfloat16 [2048, 1024], P(('dp', 'blk', 'fsdp')), may hold values from -0.125 to 0.125
- value_weight: bfloat16 [2048, 1024], P(('dp', 'blk', 'fsdp')), may hold values from -0.125 to 0.125
- output_weight: bfloat16 [2048, 2048], P(('dp', 'blk', 'fsdp')), may hold values from -0.75 to 0.75
- norm_mlp: bfloat16 [2048], P(('dp', 'blk', 'fsdp')), may hold values from 0.5 to 1.5
- gate_weight: bfloat16 [2048, 6144], P(('dp', 'blk'), 'fsdp'), may hold values from -0.125 to 0.125
- upward_weight: bfloat16 [2048, 6144], P(('dp', 'blk'), 'fsdp'), may hold values from -0.125 to 0.125
- down_weight: bfloat16 [2048, 6144], P(('dp', 'blk'), 'fsdp'), may hold values from -0.078125 to 0.078125
Outputs:
- layer_out: bfloat16 [8, 1024, 2048], P('dp', ('blk', 'fsdp'))
- input_grad: float32 [8, 1024, 2048], P('dp', ('blk', 'fsdp'))
- norm_attn_grad: float32 [2048], P(('dp', 'blk', 'fsdp'))
- query_gain_grad: float32 [128], P(('dp', 'blk', 'fsdp'))
- key_gain_grad: float32 [128], P(('dp', 'blk', 'fsdp'))
- query_weight_grad: float32 [2048, 2048], P(('dp', 'blk', 'fsdp'))
- key_weight_grad: float32 [2048, 1024], P(('dp', 'blk', 'fsdp'))
- value_weight_grad: float32 [2048, 1024], P(('dp', 'blk', 'fsdp'))
- output_weight_grad: float32 [2048, 2048], P(('dp', 'blk', 'fsdp'))
- norm_mlp_grad: float32 [2048], P(('dp', 'blk', 'fsdp'))
- gate_weight_grad: float32 [2048, 6144], P(('dp', 'blk'), 'fsdp')
- upward_weight_grad: float32 [2048, 6144], P(('dp', 'blk'), 'fsdp')
- down_weight_grad: float32 [2048, 6144], P(('dp', 'blk'), 'fsdp')
The draws below stay inside these ranges and needn't reach their ends.
Inputs may be any that keep to these rules, and one draw needn't show every extreme that they name: `doc_lengths`: each row's 4 lengths are positive and sum to 1024. In each group of 2 rows on one index of dp, one row's first document has 960 positions.
All inputs are finite; a program needn't handle non-finite values.
Results may differ from the reference program's by a relative error of at most 0.028.
Values may be sent and summed in bfloat16 or wider, within the bound.
No kernel may reach another device: no remote copies, remote signals or barrier semaphores. Data moves between devices by JAX's collectives and lax.ppermute only.
A program may use at most 512 MiB of HBM per device.

```python
import math
import jax
import jax.numpy as jnp
from jax import lax

D = 2048
HQ = 16
HK = 8
HD = 128
FF = 6144
SEQ_BLOCK = 128
SEQS = 2
NDOCS = 4
LENGTH = 1024
ROWS = 8


def draw_doc_lengths(key, part):
    key = jax.random.fold_in(key, 7)
    share_key, pick_key = jax.random.split(key)
    shares = jax.random.randint(share_key, (ROWS, NDOCS), 1000, 4000)
    spread_rows = 1 + (LENGTH - NDOCS) * shares // jnp.sum(shares, axis=1, keepdims=True)
    spread_rows = spread_rows.at[:, NDOCS - 1].add(LENGTH - jnp.sum(spread_rows, axis=1))
    remain = SEQ_BLOCK // 2
    tail_rows = 1 + (remain - NDOCS + 1) * shares[:, 1:] // jnp.sum(shares[:, 1:], axis=1, keepdims=True)
    tail_rows = tail_rows.at[:, NDOCS - 2].add(remain - jnp.sum(tail_rows, axis=1))
    long_rows = jnp.concatenate([jnp.full((ROWS, 1), LENGTH - remain, jnp.int32), tail_rows.astype(jnp.int32)], axis=1)
    chosen = jax.random.randint(pick_key, (ROWS // SEQS,), 0, SEQS)
    row_ids = jnp.arange(ROWS, dtype=jnp.int32)
    is_long = row_ids % SEQS == jnp.repeat(chosen, SEQS)
    return jnp.where(is_long[:, None], long_rows, spread_rows.astype(jnp.int32)).astype(jnp.int32)


def level_of(rng, shape, cuts, smallest, top_value):
    level = 1.0
    for dim, shards_of in cuts:
        steps = jax.random.uniform(jax.random.fold_in(jax.random.fold_in(rng, 6), dim), (shards_of,), jnp.float32, smallest / len(cuts), top_value / len(cuts))
        level = level * jnp.repeat(jnp.exp(steps), shape[dim] // shards_of).reshape((-1,) + (1,) * (len(shape) - 1 - dim))
    return level


def scatter_about(stream_key, dims, deviation, bound, pieces=(), held_as=jnp.bfloat16):
    level = level_of(stream_key, dims, pieces, -0.22, 0.18) if pieces else 1.0
    values = jax.random.normal(stream_key, dims, jnp.float32) * deviation * level
    return jnp.minimum(jnp.maximum(values, -bound), bound).astype(held_as)


def setup_inputs(seed: int = 0) -> dict:
    streams_of = jax.random.split(jax.random.key(seed), 15)
    return {
        "hidden_in": scatter_about(streams_of[0], (ROWS, LENGTH, D), 1.0, 6.0, ((0, 4), (1, 8))),
        "out_grad": scatter_about(streams_of[1], (ROWS, LENGTH, D), 1.0, 6.0, ((0, 4), (1, 8))),
        "doc_lengths": draw_doc_lengths(jax.random.fold_in(streams_of[14], 71), 0),
        "norm_attn": jnp.clip(1.0 + 0.1 * jax.random.normal(streams_of[3], (D,), jnp.float32), 0.5, 1.5).astype(jnp.bfloat16),
        "query_gain": jnp.clip(1.0 + 0.1 * jax.random.normal(streams_of[4], (HD,), jnp.float32), 0.5, 1.5).astype(jnp.bfloat16),
        "key_gain": jnp.clip(1.0 + 0.1 * jax.random.normal(streams_of[5], (HD,), jnp.float32), 0.5, 1.5).astype(jnp.bfloat16),
        "query_weight": scatter_about(streams_of[6], (D, HQ * HD), D ** -0.5, 0.125, ((0, 32),)),
        "key_weight": scatter_about(streams_of[7], (D, HK * HD), D ** -0.5, 0.125, ((0, 32),)),
        "value_weight": scatter_about(streams_of[8], (D, HK * HD), D ** -0.5, 0.125, ((0, 32),)),
        "output_weight": scatter_about(streams_of[9], (HQ * HD, D), 64 ** -0.5, 0.75, ((0, 32),)),
        "norm_mlp": jnp.clip(1.0 + 0.1 * jax.random.normal(streams_of[10], (D,), jnp.float32), 0.5, 1.5).astype(jnp.bfloat16),
        "gate_weight": scatter_about(streams_of[11], (D, FF), D ** -0.5, 0.125, ((0, 16), (1, 2))),
        "upward_weight": scatter_about(streams_of[12], (D, FF), D ** -0.5, 0.125, ((0, 16), (1, 2))),
        "down_weight": scatter_about(streams_of[13], (D, FF), FF ** -0.5, 0.078125, ((0, 16), (1, 2))),
    }


EPSILON = 1e-06
ROPE_BASE = 1000000.0
MASKED = -1e+30
HIGH = lax.Precision.HIGHEST

@jax.custom_vjp
def low(v):
    return lax.optimization_barrier(v.astype(jnp.bfloat16)).astype(jnp.float32)

@jax.custom_vjp
def low_back(v):
    return v

def low_keep(v):
    return (low(v), None)

def low_pass(kept, grad):
    return (grad,)

def back_keep(v):
    return (v, None)

def back_low(kept, grad):
    return (low(grad),)
low.defvjp(low_keep, low_pass)
low_back.defvjp(back_keep, back_low)

def normalize(values, gain):
    inverse = lax.rsqrt(lax.optimization_barrier(jnp.mean(values * values, axis=-1, keepdims=True)) + EPSILON)
    return values * inverse * gain

def rotate(values, cos_table, sine_table):
    halfway = values.shape[-1] // 2
    turned = jnp.concatenate([-values[..., halfway:], values[..., :halfway]], axis=-1)
    return values * cos_table + turned * sine_table

def placement_of(lengths, total):
    places = jnp.arange(total, dtype=jnp.int32)
    ends = jnp.cumsum(lengths).astype(jnp.int32)
    before = (ends[None, :] <= places[:, None]).astype(jnp.int32)
    document = lax.optimization_barrier(jnp.sum(before, axis=1)).astype(jnp.int32)
    doc_start = lax.optimization_barrier(jnp.sum(before * lengths[None, :], axis=1)).astype(jnp.int32)
    return (document, places - doc_start, places)

def rotary_tables(position):
    frequency = jnp.exp(jnp.arange(HD // 2, dtype=jnp.float32) * (-2.0 / HD) * math.log(ROPE_BASE))
    angles = position.astype(jnp.float32)[:, None] * frequency[None, :]
    angles = jnp.concatenate([angles, angles], axis=1)
    return (jnp.cos(angles)[:, None, :], jnp.sin(angles)[:, None, :])

def row_forward(layer_in, lengths, params):
    norm_attn, query_gain, key_gain, query_weight, key_weight, value_weight, output_weight, norm_mlp, gate_weight, upward_weight, down_weight = params
    document, position, places = placement_of(lengths, LENGTH)
    cos_table, sine_table = rotary_tables(position)
    first_norm = low(normalize(layer_in, norm_attn))
    query_raw = low_back(jnp.dot(first_norm, query_weight, precision=HIGH)).reshape(LENGTH, HQ, HD)
    key_raw = low_back(jnp.dot(first_norm, key_weight, precision=HIGH)).reshape(LENGTH, HK, HD)
    value_rows = low(low_back(jnp.dot(first_norm, value_weight, precision=HIGH))).reshape(LENGTH, HK, HD)
    query_rows = low(rotate(normalize(query_raw, query_gain), cos_table, sine_table))
    key_rows = low(rotate(normalize(key_raw, key_gain), cos_table, sine_table))
    group_size = HQ // HK
    block_rows = min(512, LENGTH)
    block_count = LENGTH // block_rows
    query_blocks = query_rows.reshape(block_count, block_rows, HK, group_size, HD)
    doc_blocks = document.reshape(block_count, block_rows)
    place_blocks = places.reshape(block_count, block_rows)
    softmax_scale = 1.0 / math.sqrt(HD)

    def attend(element):
        query_block, query_doc, query_place = element
        scores = jnp.einsum('qkgd,pkd->kgqp', query_block, key_rows, precision=HIGH) * softmax_scale
        scores = low_back(scores)
        visible = (query_doc[:, None] == document[None, :]) & (places[None, :] <= query_place[:, None])
        scores = jnp.where(visible[None, None], scores, MASKED)
        weights = low(jax.nn.softmax(scores, axis=-1))
        return jnp.einsum('kgqp,pkd->qkgd', weights, value_rows, precision=HIGH)
    mixed = lax.map(jax.checkpoint(attend), (query_blocks, doc_blocks, place_blocks))
    mixed = low(low_back(mixed.reshape(LENGTH, HQ * HD)))
    residual = layer_in + low_back(jnp.dot(mixed, output_weight, precision=HIGH))
    second_norm = low(normalize(residual, norm_mlp))
    gate_proj = low_back(jnp.dot(second_norm, gate_weight, precision=HIGH))
    upward_proj = low_back(jnp.dot(second_norm, upward_weight, precision=HIGH))
    hidden_rows = low(jax.nn.silu(gate_proj) * upward_proj)
    return residual + low_back(jnp.dot(hidden_rows, down_weight.T, precision=HIGH))

def reference(hidden_in, out_grad, doc_lengths, norm_attn, query_gain, key_gain, query_weight, key_weight, value_weight, output_weight, norm_mlp, gate_weight, upward_weight, down_weight):
    params = jax.tree.map(lambda member: member.astype(jnp.float32), (norm_attn, query_gain, key_gain, query_weight, key_weight, value_weight, output_weight, norm_mlp, gate_weight, upward_weight, down_weight))

    def one_row(totals, element):
        row_in, row_grad, lengths = element

        def forward(layer_in, weights_in):
            return row_forward(layer_in, lengths, weights_in)
        result, pullback = jax.vjp(forward, row_in.astype(jnp.float32), params)
        row_in_grad, param_grads = pullback(row_grad.astype(jnp.float32))
        totals = jax.tree.map(lambda total_part, new_part: total_part + new_part, totals, param_grads)
        return (totals, (result.astype(jnp.bfloat16), row_in_grad))
    zeros_init = jax.tree.map(jnp.zeros_like, params)
    totals, (layer_out, input_grad) = lax.scan(one_row, zeros_init, (hidden_in, out_grad, doc_lengths))
    return (layer_out, input_grad, totals[0], totals[1], totals[2], totals[3], totals[4], totals[5], totals[6], totals[7], totals[8], totals[9], totals[10])
```

```python
import functools
import math

import jax
import jax.numpy as jnp
from jax import lax
from jax.experimental import pallas as pl
from jax.experimental.pallas import tpu as pltpu
from jax.sharding import PartitionSpec as P

EPSILON = 1e-06
ROPE_BASE = 1000000.0
MASKED = -1e30
BF = jnp.bfloat16
F32 = jnp.float32
EVERY = ("dp", "blk", "fsdp")


def running_ends(lengths):
    parts = [lengths[..., :1]]
    for index in range(1, lengths.shape[-1]):
        parts.append(parts[-1] + lengths[..., index : index + 1])
    return jnp.concatenate(parts, axis=-1)


SWAP_X = [(0, 2), (2, 0), (1, 3), (3, 1)]
SWAP_C = [(0, 1), (1, 0), (2, 3), (3, 2)]
SWAP_Y = [(0, 1), (1, 0)]
BLOCK = 128
PIECES = 8


def over_x(value):
    return lax.ppermute(value, "dp", SWAP_X)


def over_c(value):
    return lax.ppermute(value, "dp", SWAP_C)


def over_y(value):
    return lax.ppermute(value, "fsdp", SWAP_Y)


def after(value, *before):
    return lax.optimization_barrier((value, *before))[0]


def sum_low(*parts):
    return functools.reduce(lambda a, b: a + b, [p.astype(F32) for p in parts]).astype(BF)


def by_bit(bit, zero, one):
    return jnp.where(bit == 1, one, zero)


def pick(value, index, axis):
    return lax.dynamic_index_in_dim(value, index, axis, keepdims=False)


def flip_where(bit, value, axis):
    first, second = jnp.split(value, 2, axis)
    return jnp.where(bit == 1, jnp.concatenate([second, first], axis), value)


def together(*values):
    return lax.optimization_barrier(values)


def layer_gather(low, high, core_after=()):
    low_x, high_y = together(over_x(low), over_y(high))
    low_row, high_row = together(jnp.concatenate([low, low_x]), jnp.concatenate([high, high_y]))
    low_both, high_both = together(over_y(low_row), over_x(high_row))
    near = [low_row, low_both, high_row, high_both]
    last = [after(piece, *core_after) if core_after else piece for piece in (low_both, high_both)]
    sent = [low_row, last[0], high_row, last[1]]
    return near + [over_c(piece) for piece in sent], (low_row, high_row)


def layer_scatter(product, core_after=()):
    sent_low, sent_high = product(1024, 1536), product(1536, 2048)
    here = product(0, 1024, sent_low, sent_high)
    far_low, far_high = together(
        over_c(after(sent_low, *core_after)), over_c(after(sent_high, *core_after))
    )
    second = together(sum_low(here[256:512], far_low[256:]), sum_low(here[768:], far_high[256:]))
    low_back, high_back = together(over_y(second[0]), over_x(second[1]))
    third = together(
        sum_low(here[128:256], far_low[128:256], low_back[128:]),
        sum_low(here[640:768], far_high[128:256], high_back[128:]),
    )
    low_last, high_last = together(over_x(third[0]), over_y(third[1]))
    parts = (
        (here[:128], far_low[:128], low_back[:128], low_last),
        (here[512:640], far_high[:128], high_back[:128], high_last),
    )
    return parts, here, second, third


def product_of(rows, matrix, dims, more=None):
    def product(first, last, *before):
        part = rows[first:last]
        part = after(part, *before) if before else part
        out = lax.dot_general(part, matrix, dims, preferred_element_type=F32)
        return (out if more is None else out + more[first].astype(F32)).astype(BF)

    return product


def total_of(parts):
    return functools.reduce(lambda a, b: a + b, [p.astype(F32) for p in parts])


def blk_gather(own):
    return lax.all_gather(own, "blk", axis=0, tiled=True)


def blk_scatter(partial):
    return lax.psum_scatter(partial, "blk", scatter_dimension=0, tiled=True)


def swap_z(value, step):
    return lax.ppermute(value, "blk", [(z, z ^ step) for z in range(4)])


def small_gather_z(value, z):
    for bit, step in ((z % 2, 1), (z // 2, 2)):
        value = flip_where(bit, jnp.stack([value, swap_z(value, step)]), 0)
    return value


def small_gather(value, coords):
    x_bit, c_bit, y_bit = coords
    for bit, move in ((y_bit, over_y), (c_bit, over_c), (x_bit, over_x)):
        value = flip_where(bit, jnp.stack([value, move(value)]), 0)
    return value.reshape(2, 2, 2, 4, -1)


def small_scatter(value, coords, z):
    x_bit, c_bit, y_bit = coords
    value = value.reshape(2, 2, 2, 2, 2, -1)
    moves = (
        (z // 2, functools.partial(swap_z, step=2), 2),
        (z % 2, functools.partial(swap_z, step=1), 2),
        (x_bit, over_x, 0),
        (c_bit, over_c, 0),
        (y_bit, over_y, 0),
    )
    for bit, move, axis in moves:
        value = pick(value, bit, axis) + move(pick(value, 1 - bit, axis))
    return value


def width_blocks(value):
    step = value.shape[-1] // 16
    return [value[..., i * step : (i + 1) * step] for i in range(16)]


def model_order(value):
    blocks = width_blocks(value)
    return jnp.concatenate([blocks[j * 4 + i] for i in range(4) for j in range(4)], axis=-1)


def trade(value, bit, move, axis):
    keep, got = pick(value, bit, axis), move(pick(value, 1 - bit, axis))
    return by_bit(bit, jnp.stack([keep, got], axis), jnp.stack([got, keep], axis))


def join(keep, got, bit, axis):
    return by_bit(bit, jnp.stack([keep, got], axis), jnp.stack([got, keep], axis))


def row_moves():
    first, second = [], []
    for d in range(4):
        for z in range(4):
            for y in range(2):
                source = d * 8 + z * 2 + y
                target = (d // 2) * 2 + z // 2
                first.append((source, target * 8 + (2 * (d % 2) + z % 2) * 2 + y))
                second.append((source, target * 8 + (2 * (d % 2) + 1 - z % 2) * 2 + y))
    return first, second


def sort_width(read, write, width):
    step = width // 16
    for i in range(4):
        for j in range(4):
            write(slice((i * 4 + j) * step, (i * 4 + j + 1) * step), read(slice((j * 4 + i) * step, (j * 4 + i + 1) * step)))


def send_rows_kernel(odd_ref, value_ref, first_ref, second_ref):
    odd = odd_ref[0]
    for out, at in ((first_ref, odd), (second_ref, 1 - odd)):

        def write(cols, value, out=out):
            out[:, cols] = value

        sort_width(lambda cols, at=at: value_ref[at, :, cols], write, out.shape[1])


def send_rows(value, odd):
    shape = jax.ShapeDtypeStruct(value.shape[1:], value.dtype)
    return pl.pallas_call(
        send_rows_kernel,
        in_specs=[pl.BlockSpec(memory_space=pltpu.SMEM), pl.BlockSpec(memory_space=pltpu.VMEM)],
        out_specs=[pl.BlockSpec(memory_space=pltpu.VMEM)] * 2,
        out_shape=[shape, shape],
    )(odd.reshape(1), value)


def keep_rows_kernel(odd_ref, first_ref, second_ref, out_ref):
    odd = odd_ref[0]
    for got, at in ((first_ref, odd), (second_ref, 1 - odd)):

        def write(cols, value, at=at):
            out_ref[at, :, cols] = value.astype(out_ref.dtype)

        sort_width(lambda cols, got=got: got[:, cols], write, got.shape[1])


def keep_rows(first, second, odd, dtype):
    return pl.pallas_call(
        keep_rows_kernel,
        in_specs=[pl.BlockSpec(memory_space=pltpu.SMEM)] + [pl.BlockSpec(memory_space=pltpu.VMEM)] * 2,
        out_specs=pl.BlockSpec(memory_space=pltpu.VMEM),
        out_shape=jax.ShapeDtypeStruct((2, *first.shape), dtype),
    )(odd.reshape(1), first, second)


def sort_kernel(value_ref, out_ref):
    def write(cols, value):
        out_ref[:, cols] = value.astype(out_ref.dtype)

    sort_width(lambda cols: value_ref[:, cols], write, value_ref.shape[1])


def sort_model(value, dtype):
    return pl.pallas_call(
        sort_kernel,
        in_specs=[pl.BlockSpec(memory_space=pltpu.VMEM)],
        out_specs=pl.BlockSpec(memory_space=pltpu.VMEM),
        out_shape=jax.ShapeDtypeStruct(value.shape, dtype),
    )(value)


def rows_in(sent, odd):
    moves = row_moves()
    got_first = lax.ppermute(sent[0], EVERY, moves[0])
    got_second = lax.ppermute(sent[1], EVERY, moves[1])
    return by_bit(odd, got_first, got_second), by_bit(odd, got_second, got_first)


def rows_out(low, high, odd, dtype):
    moves = row_moves()
    got_first = lax.ppermute(by_bit(odd, low, high), EVERY, [(b, a) for a, b in moves[0]])
    got_second = lax.ppermute(by_bit(odd, high, low), EVERY, [(b, a) for a, b in moves[1]])
    return keep_rows(got_first, got_second, odd, dtype)


def block_rows(scalars, row, block):
    c_bit, y_bit = scalars[0], scalars[1]
    far_c = jnp.where(c_bit == (block >> 2), 0, 1)
    far_y = jnp.where(y_bit == (block & 1), 0, 1)
    if (block >> 1) & 1:
        at = far_c * 8 + 4 + row * 2 + far_y
    else:
        at = far_c * 8 + far_y * 2 + row
    return pl.ds(pl.multiple_of(at * BLOCK, BLOCK), BLOCK)


def swap_halves(value):
    return pltpu.roll(value, value.shape[-1] // 2, 1)


def head_forward(raw, gain, cos, sine):
    inverse = lax.rsqrt(jnp.mean(raw * raw, axis=-1, keepdims=True) + EPSILON)
    scaled = raw * inverse * gain
    return scaled * cos + swap_halves(scaled) * sine


def head_backward(grad, raw, gain, cos, sine):
    inverse = lax.rsqrt(jnp.mean(raw * raw, axis=-1, keepdims=True) + EPSILON)
    unit = raw * inverse
    back = grad * cos + swap_halves(grad * sine)
    gain_grad = jnp.sum(back * unit, axis=0, keepdims=True)
    scaled = back * gain
    return inverse * (scaled - unit * jnp.mean(scaled * unit, axis=-1, keepdims=True)), gain_grad


def visible_pairs(scalars, row, first_query, queries, keys, docs):
    place = first_query + lax.broadcasted_iota(jnp.int32, (queries, 1), 0)
    start = jnp.zeros_like(place)
    for doc in range(docs - 1):
        end = scalars[2 + row * docs + doc]
        start = jnp.where(place >= end, end, start)
    key_place = lax.broadcasted_iota(jnp.int32, (queries, keys), 1)
    return (key_place >= start) & (key_place <= place)


def fetch(pieces, held, sems, base=0):
    size = held.shape[0] // len(pieces)
    return [
        pltpu.make_async_copy(piece, held.at[pl.ds(i * size, size), :], sems.at[base + i])
        for i, piece in enumerate(pieces)
    ]


def load_row(scalars, row, raw_ref, cos_ref, sine_ref, gain_ref, q_s, k_s, v_s, groups, blocks):
    width = 128
    for block in range(blocks):
        rel = block_rows(scalars, row, block)
        rows = slice(block * BLOCK, block * BLOCK + BLOCK)
        cos, sine = cos_ref[0, rows, :], sine_ref[0, rows, :]
        for g in range(groups):
            raw = raw_ref[rel, g * width : (g + 1) * width]
            q_s[rows, g * width : (g + 1) * width] = head_forward(
                raw, gain_ref[0:1, :], cos, sine
            ).astype(BF)
        raw = raw_ref[rel, groups * width : (groups + 1) * width]
        k_s[rows, :] = head_forward(raw, gain_ref[1:2, :], cos, sine).astype(BF)
        v_s[rows, :] = raw_ref[rel, (groups + 1) * width : (groups + 2) * width].astype(BF)


ROWS_C = (((1,), (1,)), ((), ()))
COLS_C = (((0,), (0,)), ((), ()))


def attend_kernel(scalars, cos_ref, sine_ref, gain_ref, *refs, groups, docs, step):
    raw_s, mix_ref, q_s, k_s, v_s = refs
    row = pl.program_id(0)
    total = k_s.shape[0]
    load_row(scalars, row, raw_s, cos_ref, sine_ref, gain_ref, q_s, k_s, v_s, groups, total // BLOCK)
    scale = 1.0 / math.sqrt(128)
    for first in range(0, total, step):
        keys = first + step
        visible = visible_pairs(scalars, row, first, step, keys, docs)
        for g in range(groups):
            query = q_s[first : first + step, g * 128 : (g + 1) * 128]
            scores = lax.dot_general(query, k_s[:keys, :], ROWS_C, preferred_element_type=F32) * scale
            scores = jnp.where(visible, scores, MASKED)
            weights = jnp.exp(scores - jnp.max(scores, axis=-1, keepdims=True))
            norm = jnp.sum(weights, axis=-1, keepdims=True)
            mixed = jnp.dot(weights.astype(BF), v_s[:keys, :], preferred_element_type=F32) / norm
            for part in range(step // BLOCK):
                rel = block_rows(scalars, row, first // BLOCK + part)
                mix_ref[rel, g * 128 : (g + 1) * 128] = mixed[part * BLOCK : (part + 1) * BLOCK].astype(BF)


def attend_back_kernel(scalars, cos_ref, sine_ref, gain_ref, *refs, groups, docs, step):
    raw_s, dmix_s, draw_ref, dgain_ref, q_s, k_s, v_s, dk_s, dv_s = refs
    row = pl.program_id(0)
    total = k_s.shape[0]
    load_row(scalars, row, raw_s, cos_ref, sine_ref, gain_ref, q_s, k_s, v_s, groups, total // BLOCK)
    scale = 1.0 / math.sqrt(128)
    dk_s[...] = jnp.zeros_like(dk_s)
    dv_s[...] = jnp.zeros_like(dv_s)
    query_gain = jnp.zeros((1, 128), F32)
    for first in range(0, total, step):
        keys = first + step
        visible = visible_pairs(scalars, row, first, step, keys, docs)
        order = [block_rows(scalars, row, first // BLOCK + part) for part in range(step // BLOCK)]
        for g in range(groups):
            cols = slice(g * 128, (g + 1) * 128)
            query = q_s[first : first + step, cols]
            dmix = jnp.concatenate([dmix_s[rel, cols] for rel in order], axis=0)
            scores = lax.dot_general(query, k_s[:keys, :], ROWS_C, preferred_element_type=F32) * scale
            scores = jnp.where(visible, scores, MASKED)
            weights = jnp.exp(scores - jnp.max(scores, axis=-1, keepdims=True))
            probs = weights / jnp.sum(weights, axis=-1, keepdims=True)
            dprobs = lax.dot_general(dmix, v_s[:keys, :], ROWS_C, preferred_element_type=F32)
            delta = jnp.sum(probs * dprobs, axis=-1, keepdims=True)
            dscores = (probs * (dprobs - delta)).astype(BF)
            dquery = jnp.dot(dscores, k_s[:keys, :], preferred_element_type=F32) * scale
            dk_s[:keys, :] += lax.dot_general(dscores, query, COLS_C, preferred_element_type=F32)
            dv_s[:keys, :] += lax.dot_general(probs.astype(BF), dmix, COLS_C, preferred_element_type=F32)
            for part, rel in enumerate(order):
                rows = slice(first + part * BLOCK, first + (part + 1) * BLOCK)
                draw, gain_part = head_backward(
                    dquery[part * BLOCK : (part + 1) * BLOCK], raw_s[rel, cols], gain_ref[0:1, :],
                    cos_ref[0, rows, :], sine_ref[0, rows, :],
                )
                draw_ref[rel, cols] = draw.astype(BF)
                query_gain += gain_part
    key_gain = jnp.zeros((1, 128), F32)
    cols = slice(groups * 128, (groups + 1) * 128)
    for block in range(total // BLOCK):
        rel = block_rows(scalars, row, block)
        rows = slice(block * BLOCK, (block + 1) * BLOCK)
        draw, gain_part = head_backward(
            dk_s[rows, :] * scale, raw_s[rel, cols], gain_ref[1:2, :], cos_ref[0, rows, :], sine_ref[0, rows, :]
        )
        draw_ref[rel, cols] = draw.astype(BF)
        draw_ref[rel, (groups + 1) * 128 : (groups + 2) * 128] = dv_s[rows, :].astype(BF)
        key_gain += gain_part
    dgain_ref[0, :, :] = jnp.concatenate([query_gain, key_gain, jnp.zeros((6, 128), F32)], axis=0)


ATTEND_STEP = 256


def attend(scalars, raw, cos, sine, gains, groups, docs, dmix=None):
    total, width = cos.shape[1], raw.shape[1]
    by_row = pl.BlockSpec((1, total, 128), lambda r, s: (r, 0, 0))
    back = dmix is not None
    given = [raw, dmix] if back else [raw]
    once = lambda columns: pl.BlockSpec((2 * total, columns), lambda r, s: (0, 0))
    out_specs = [once(width if back else groups * 128)]
    out_shape = [jax.ShapeDtypeStruct((2 * total, width if back else groups * 128), BF)]
    if back:
        out_specs.append(pl.BlockSpec((1, 8, 128), lambda r, s: (r, 0, 0)))
        out_shape.append(jax.ShapeDtypeStruct((2, 8, 128), F32))
    scratch = [
        pltpu.VMEM((total, groups * 128), BF),
        pltpu.VMEM((total, 128), BF),
        pltpu.VMEM((total, 128), BF),
    ]
    if back:
        scratch += [pltpu.VMEM((total, 128), F32), pltpu.VMEM((total, 128), F32)]
    return pl.pallas_call(
        functools.partial(
            attend_back_kernel if back else attend_kernel, groups=groups, docs=docs, step=ATTEND_STEP
        ),
        grid_spec=pltpu.PrefetchScalarGridSpec(
            num_scalar_prefetch=1,
            grid=(2,),
            in_specs=[by_row, by_row, pl.BlockSpec((8, 128), lambda r, s: (0, 0))]
            + [once(part.shape[1]) for part in given],
            out_specs=out_specs,
            scratch_shapes=scratch,
        ),
        out_shape=out_shape,
        compiler_params=pltpu.CompilerParams(vmem_limit_bytes=40 * 2**20),
        cost_estimate=pl.CostEstimate(
            flops=groups * total * total * 128 * 2 * (5 if back else 2) * 2 * 5 // 8,
            bytes_accessed=(40 if back else 12) * 2**20,
            transcendentals=groups * total * total * 2,
        ),
    )(scalars, cos, sine, gains, *given)


def pieces_kernel(matrix_ref, *refs, dims):
    pieces, (out_ref, whole_ref, held, sems, out_sem) = refs[:PIECES], refs[PIECES:]
    copies = fetch(pieces, held, sems)
    for copy in copies:
        copy.start()
    size = held.shape[0] // PIECES
    for at, copy in enumerate(copies):
        copy.wait()
        rows = slice(at * size, (at + 1) * size)
        out_ref[rows, :] = lax.dot_general(
            held[rows, :], matrix_ref[...], dims, preferred_element_type=F32
        ).astype(out_ref.dtype)
    out = pltpu.make_async_copy(held, whole_ref, out_sem)
    out.start()
    out.wait()


def pieces_dot(pieces, matrix, dims, dtype):
    rows, width = pieces[0].shape
    columns = matrix.shape[1 - dims[0][1][0]]
    vmem, anywhere = pl.BlockSpec(memory_space=pltpu.VMEM), pl.BlockSpec(memory_space=pl.ANY)
    return pl.pallas_call(
        functools.partial(pieces_kernel, dims=dims),
        in_specs=[vmem] + [anywhere] * PIECES,
        out_specs=[vmem, anywhere],
        out_shape=[
            jax.ShapeDtypeStruct((PIECES * rows, columns), dtype),
            jax.ShapeDtypeStruct((PIECES * rows, width), BF),
        ],
        scratch_shapes=[
            pltpu.VMEM((PIECES * rows, width), BF),
            pltpu.SemaphoreType.DMA((PIECES,)),
            pltpu.SemaphoreType.DMA,
        ],
        compiler_params=pltpu.CompilerParams(vmem_limit_bytes=32 * 2**20),
        cost_estimate=pl.CostEstimate(
            flops=2 * PIECES * rows * width * columns,
            bytes_accessed=4 * PIECES * rows * width + 4 * PIECES * rows * columns,
            transcendentals=0,
        ),
    )(matrix, *pieces)


UNIT_TILE = 256
TOKEN_TILE = 512


def units_kernel(both_ref, down_ref, *refs, given):
    normed, tops = refs[:given], refs[given : 2 * given]
    hidden_ref, dboth_ref = refs[2 * given : 2 * given + 2]
    *wholes, normed_s, top_s, sems, out_sems = refs[2 * given + 2 :]
    at = pl.program_id(0)
    last = pl.num_programs(0) - 1
    size = normed_s.shape[0] // PIECES
    if given == 1:
        normed, tops = ([r[0].at[pl.ds(i * size, size), :] for i in range(PIECES)] for r in (normed, tops))
    copies = fetch(normed, normed_s, sems), fetch(tops, top_s, sems, PIECES)
    outs = [
        pltpu.make_async_copy(held, whole, out_sems.at[i])
        for i, (held, whole) in enumerate(zip((normed_s, top_s), wholes))
    ]

    @pl.when(at == 0)
    def _():
        for one, other in zip(*copies, strict=True):
            one.start()
            other.start()

    per = TOKEN_TILE // size
    for tile in range(normed_s.shape[0] // TOKEN_TILE):

        @pl.when(at == 0)
        def _(tile=tile):
            for piece in range(tile * per, (tile + 1) * per):
                copies[0][piece].wait()
                copies[1][piece].wait()

        rows = slice(tile * TOKEN_TILE, (tile + 1) * TOKEN_TILE)
        both = jnp.dot(normed_s[rows, :], both_ref[...], preferred_element_type=F32)
        gate, upward = both[:, :UNIT_TILE], both[:, UNIT_TILE:]
        dhidden = jnp.dot(top_s[rows, :], down_ref[...], preferred_element_type=F32)
        logistic = 1.0 / (1.0 + jnp.exp(-gate))
        swish = gate * logistic
        hidden_ref[rows, :] = (swish * upward).astype(BF)
        dgate = dhidden * upward * (logistic * (1.0 + gate * (1.0 - logistic)))
        dboth_ref[rows, :UNIT_TILE] = dgate.astype(BF)
        dboth_ref[rows, UNIT_TILE:] = (dhidden * swish).astype(BF)

    if outs:

        @pl.when(at == 0)
        def _():
            for out in outs:
                out.start()

        @pl.when(at == last)
        def _():
            for out in outs:
                out.wait()


def units_pass(normed, tops, mat):
    given = len(normed)
    width, units = mat.shape[0], mat.shape[1] // 3
    tiles = units // UNIT_TILE
    tokens = given * normed[0].shape[0]
    anywhere = pl.BlockSpec(memory_space=pl.ANY)
    whole = jax.ShapeDtypeStruct((tokens, width), BF)
    wholes = 0 if given == 1 else 2
    return pl.pallas_call(
        functools.partial(units_kernel, given=given),
        grid=(tiles,),
        in_specs=[
            pl.BlockSpec((width, 2 * UNIT_TILE), lambda i: (0, i)),
            pl.BlockSpec((width, UNIT_TILE), lambda i: (0, 2 * tiles + i)),
        ]
        + [anywhere] * (2 * given),
        out_specs=[
            pl.BlockSpec((tokens, UNIT_TILE), lambda i: (0, i)),
            pl.BlockSpec((tokens, 2 * UNIT_TILE), lambda i: (0, i)),
        ]
        + [anywhere] * wholes,
        out_shape=[
            jax.ShapeDtypeStruct((tokens, units), BF),
            jax.ShapeDtypeStruct((tokens, 2 * units), BF),
        ]
        + [whole] * wholes,
        scratch_shapes=[
            pltpu.VMEM((tokens, width), BF),
            pltpu.VMEM((tokens, width), BF),
            pltpu.SemaphoreType.DMA((2 * PIECES,)),
            pltpu.SemaphoreType.DMA((2,)),
        ],
        compiler_params=pltpu.CompilerParams(vmem_limit_bytes=48 * 2**20),
        cost_estimate=pl.CostEstimate(
            flops=2 * tokens * width * units * 3,
            bytes_accessed=4 * tokens * width * 2 + 6 * width * units + 6 * tokens * units,
            transcendentals=tokens * units,
        ),
    )(mat, mat, *normed, *tops)


def norm_inverse(values):
    return lax.rsqrt(jnp.mean(values * values, axis=-1, keepdims=True) + EPSILON)


def norm_back(grad, unit, inverse, gain):
    scaled = grad * gain
    return inverse * (scaled - unit * jnp.mean(scaled * unit, axis=-1, keepdims=True))


def wgrad(rows, columns):
    return lax.dot_general(rows, columns, COLS_C, preferred_element_type=F32).astype(BF)


CHUNKS = ((0, 2), (2, 3))


def layer_shards(
    hidden_in, out_grad, doc_lengths, norm_attn, query_gain, key_gain, query_weight, key_weight,
    value_weight, output_weight, norm_mlp, gate_weight, upward_weight, down_weight,
):
    d, z, y = lax.axis_index("dp"), lax.axis_index("blk"), lax.axis_index("fsdp")
    x_bit, c_bit, odd = d // 2, d % 2, z % 2
    coords = (x_bit, c_bit, y)
    width = hidden_in.shape[-1]
    docs = doc_lengths.shape[1]
    head = query_gain.shape[0] * 32
    groups = query_weight.shape[1] // key_weight.shape[1]
    total = hidden_in.shape[1] * 8
    hidden_units = gate_weight.shape[1]
    share = width // 32
    transposed = (((1,), (1,)), ((), ()))
    plain = (((1,), (0,)), ((), ()))

    small = jnp.concatenate(
        [v.astype(F32) for v in (norm_attn, norm_mlp, query_gain, key_gain)]
        + [doc_lengths.astype(F32).reshape(-1)]
    )
    small_z = small_gather_z(small, z)
    tokens = rows_in(send_rows(after(hidden_in, small_z), odd), odd)
    small_all = small_gather(small_z, coords)
    top_own = rows_in(send_rows(after(out_grad, *tokens), odd), odd)

    pieces = jnp.concatenate(
        [w.reshape(share, 8, -1) for w in (query_weight, key_weight, value_weight)], axis=-1
    )
    pieces = jnp.transpose(pieces, (1, 0, 2)).reshape(2, 2, 2, share, -1)
    pieces = trade(pieces, x_bit, over_x, 0)
    pieces = trade(pieces, y, over_y, 2)
    qkv_own = trade(pieces, c_bit, over_c, 1)

    n_attn, n_head = norm_attn.shape[0], query_gain.shape[0]
    by_device = jnp.transpose(small_all, (0, 1, 3, 2, 4)).reshape(32, -1)
    by_blk = jnp.transpose(small_all, (3, 0, 1, 2, 4)).reshape(32, -1)
    gain_attn = by_blk[:, :n_attn].reshape(-1)
    gain_mlp = by_blk[:, n_attn : 2 * n_attn].reshape(-1)
    gain_query = by_device[:, 2 * n_attn : 2 * n_attn + n_head].reshape(-1)
    gain_key = by_device[:, 2 * n_attn + n_head : 2 * n_attn + 2 * n_head].reshape(-1)
    lengths = by_device[::8, 2 * n_attn + 2 * n_head :].astype(jnp.int32).reshape(4, 2, docs)
    ends_all = running_ends(lengths)
    ends = jnp.stack(
        [ends_all[(x_bit ^ dx) * 2 + z // 2, odd] for dx in range(2)]
    )
    place = jnp.arange(total, dtype=jnp.int32)
    start = jnp.zeros((2, total), jnp.int32)
    for doc in range(docs - 1):
        start = jnp.where(place[None] >= ends[:, doc : doc + 1], ends[:, doc : doc + 1], start)
    frequency = jnp.exp(
        jnp.arange(head // 2, dtype=F32) * (-2.0 / head) * math.log(ROPE_BASE)
    )
    angles = (place[None] - start).astype(F32)[..., None] * frequency
    cos_half, sine_half = jnp.cos(angles), jnp.sin(angles)
    cos_table = jnp.concatenate([cos_half, cos_half], axis=-1)
    sine_table = jnp.concatenate([-sine_half, sine_half], axis=-1)
    scalars = jnp.concatenate([jnp.stack([c_bit, y]), ends.reshape(-1)]).astype(jnp.int32)
    head_gains = jnp.concatenate(
        [gain_query[None], gain_key[None], jnp.zeros((6, head), F32)], axis=0
    )

    quarter = hidden_units // 4
    by_quarter = [w.reshape(-1, 4, quarter // UNIT_TILE, UNIT_TILE) for w in (gate_weight, upward_weight, down_weight)]
    weight_pieces = []
    for first, last in CHUNKS:
        gates, upwards, downs = (w[:, :, first:last] for w in by_quarter)
        piece = jnp.concatenate(
            [jnp.stack([gates, upwards], axis=3).reshape(*gates.shape[:2], -1), downs.reshape(*gates.shape[:2], -1)],
            axis=-1,
        )
        weight_pieces.append(jnp.transpose(piece, (1, 0, 2)).reshape(2, 2, piece.shape[0], -1))

    def layer_weights(piece, *before):
        half = over_x(after(pick(piece, 1 - x_bit, 0), *before))
        half = join(pick(piece, x_bit, 0), half, x_bit, 0)
        return trade(half, c_bit, over_c, 1).reshape(width // 4, -1)

    owns = [layer_weights(weight_pieces[0], qkv_own, small_all)]
    qkv_own = after(qkv_own, *top_own)
    qkv_mat = blk_gather(qkv_own.reshape(8 * share, -1))
    out_all = blk_gather(after(output_weight, qkv_own)).reshape(2, 2, share, width)

    tokens = [after(t, small_all, owns[0]) for t in tokens]
    layer_in = [t.astype(F32) for t in tokens]
    inverse_attn = [norm_inverse(t) for t in layer_in]
    unit_attn = [t * i for t, i in zip(layer_in, inverse_attn, strict=True)]
    normed1, _ = layer_gather(*[(u * gain_attn).astype(BF) for u in unit_attn])
    owns += [layer_weights(piece, normed1[1], normed1[3]) for piece in weight_pieces[1:]]
    mats = [blk_gather(after(own, qkv_own)) for own in owns]
    tops, top_rows = layer_gather(*[after(t, normed1[1], normed1[3]) for t in top_own])
    raw, normed1_all = pieces_dot(normed1, after(qkv_mat, owns[1], *top_rows), plain, F32)
    raw = after(raw, tops[1], tops[3])
    out_all = trade(out_all, y, over_y, 0)
    out_mat = sort_model(jnp.swapaxes(out_all, 0, 1).reshape(-1, width), BF)
    (mix,) = attend(scalars, raw, cos_table, sine_table, head_gains, groups, docs)
    mixed, *_ = layer_scatter(product_of(mix, out_mat, plain))
    residual = [t + total_of(parts) for t, parts in zip(layer_in, mixed, strict=True)]
    inverse_mlp = [norm_inverse(t) for t in residual]
    unit_mlp = [t * i for t, i in zip(residual, inverse_mlp, strict=True)]
    normed2, _ = layer_gather(*[after((u * gain_mlp).astype(BF), *tops) for u in unit_mlp])

    hiddens, dboths, boths, downs, down_wgrads, both_wgrads = [], [], [], [], [], []
    dnormed2_part = mlp_part = None
    normed2_all = top_all = None
    for (first, last), mat in zip(CHUNKS, mats, strict=True):
        units = (last - first) * UNIT_TILE
        boths.append(mat[:, : 2 * units])
        downs.append(mat[:, 2 * units :])
        if normed2_all is None:
            hidden, dboth, normed2_all, top_all = units_pass(normed2, tops, mat)
        else:
            normed2_all = after(normed2_all, *down_wgrads, *both_wgrads, *dnormed2_part.values())
            hidden, dboth = units_pass([normed2_all], [top_all], mat)
        hiddens.append(hidden)
        dboths.append(dboth)
        if last != CHUNKS[-1][1]:
            both_wgrads.append(wgrad(normed2_all, dboth))
            down_wgrads.append(wgrad(top_all, after(hidden, both_wgrads[-1])))
            part = product_of(after(dboth, down_wgrads[-1]), boths[-1], transposed, dnormed2_part)
            dnormed2_part = {1024: part(1024, 1536), 1536: part(1536, 2048), 0: part(0, 1024)}
    dnormed2, here, second, third = layer_scatter(
        product_of(dboths[-1], boths[-1], transposed, dnormed2_part)
    )
    dnormed2 = [total_of(parts) for parts in dnormed2]
    both_wgrads.append(wgrad(after(normed2_all, here), dboths[-1]))
    down_wgrads.append(wgrad(top_all, after(hiddens[-1], *second)))

    gain_mlp_grad = sum(jnp.sum(g * u, axis=0) for g, u in zip(dnormed2, unit_mlp, strict=True))
    dresidual = [
        t.astype(F32) + norm_back(g, u, i, gain_mlp)
        for t, g, u, i in zip(top_own, dnormed2, unit_mlp, inverse_mlp, strict=True)
    ]
    both_last, down_last = both_wgrads[-1], down_wgrads[-1]
    both_wgrads = [blk_scatter(part) for part in both_wgrads]
    down_wgrads = [blk_scatter(part) for part in down_wgrads]
    for hidden, down in zip(hiddens[:-1], downs[:-1], strict=True):
        part = product_of(after(hidden, *second), down, transposed, mlp_part)
        mlp_part = {1024: part(1024, 1536), 1536: part(1536, 2048), 0: part(0, 1024)}
    mlp_product = product_of(after(hiddens[-1], *third), downs[-1], transposed, mlp_part)
    mlp_product = {first: mlp_product(first, last) for first, last in ((1024, 1536), (1536, 2048), (0, 1024))}
    dres, _ = layer_gather(
        *[after(t.astype(BF), both_last, down_last) for t in dresidual], (*mlp_product.values(),)
    )
    mlp_out, _, second, _ = layer_scatter(lambda first, *_: mlp_product[first], (dres[1], dres[3]))
    layer_out = [(t + total_of(parts)).astype(BF) for t, parts in zip(residual, mlp_out, strict=True)]
    dmix, dres_all = pieces_dot(dres, out_mat, transposed, BF)
    dmix = after(dmix, *second, *both_wgrads[:-1], *down_wgrads[:-1])
    draw, dgains = attend(scalars, raw, cos_table, sine_table, head_gains, groups, docs, dmix)
    dnormed1, here, second, third = layer_scatter(product_of(draw, qkv_mat, transposed))
    dnormed1 = [total_of(parts) for parts in dnormed1]
    qkv_wgrad = wgrad(normed1_all, after(draw, here))
    out_wgrad = wgrad(mix, after(dres_all, *second))
    out_wgrad = trade(out_wgrad.reshape(2, 2, share, width), y, over_y, 1)
    out_wgrad = jnp.swapaxes(out_wgrad, 0, 1).reshape(4 * share, width)
    qkv_wgrad = blk_scatter(after(qkv_wgrad, *both_wgrads, *down_wgrads))
    out_wgrad = blk_scatter(after(out_wgrad, *both_wgrads, *down_wgrads))
    out_wgrad = sort_model(out_wgrad, F32)
    layer_out = rows_out(*[after(t, *third) for t in layer_out], odd, BF)

    swapped = []
    for own in (*both_wgrads, *down_wgrads):
        own = after(own, *third).reshape(2, 2, width // 16, -1)
        own = trade(trade(own, c_bit, over_c, 1), x_bit, over_x, 0)
        swapped.append(own.reshape(4, width // 16, -1))
    gate_parts, upward_parts, down_parts = [], [], []
    for q in range(4):
        for at, (first, last) in enumerate(CHUNKS):
            for tile in range(last - first):
                cut = lambda i: slice(i * UNIT_TILE, (i + 1) * UNIT_TILE)
                gate_parts.append(swapped[at][q][:, cut(2 * tile)])
                upward_parts.append(swapped[at][q][:, cut(2 * tile + 1)])
                down_parts.append(swapped[len(CHUNKS) + at][q][:, cut(tile)])
    gate_wgrad, upward_wgrad, down_wgrad = (
        jnp.concatenate(parts, axis=1).astype(F32) for parts in (gate_parts, upward_parts, down_parts)
    )
    qkv_wgrad = qkv_wgrad.reshape(2, 2, 2, share, -1)
    qkv_wgrad = trade(trade(trade(qkv_wgrad, c_bit, over_c, 1), y, over_y, 2), x_bit, over_x, 0)
    qkv_wgrad = qkv_wgrad.reshape(8, share, -1)
    q_cols = groups * head
    query_wgrad = jnp.concatenate([qkv_wgrad[i][:, :q_cols] for i in range(8)], axis=1).astype(F32)
    key_wgrad = jnp.concatenate([qkv_wgrad[i][:, q_cols : q_cols + head] for i in range(8)], axis=1).astype(F32)
    value_wgrad = jnp.concatenate([qkv_wgrad[i][:, q_cols + head :] for i in range(8)], axis=1).astype(F32)

    gain_attn_grad = sum(jnp.sum(g * u, axis=0) for g, u in zip(dnormed1, unit_attn, strict=True))
    input_grad = [
        t + norm_back(g, u, i, gain_attn)
        for t, g, u, i in zip(dresidual, dnormed1, unit_attn, inverse_attn, strict=True)
    ]
    input_grad = rows_out(*[t.astype(BF) for t in input_grad], odd, F32)

    dgains = jnp.sum(dgains, axis=0)
    small_grads = jnp.concatenate(
        [
            model_order(gain_attn_grad).reshape(32, -1),
            model_order(gain_mlp_grad).reshape(32, -1),
            dgains[0].reshape(32, -1),
            dgains[1].reshape(32, -1),
        ],
        axis=1,
    )
    small_grads = small_scatter(small_grads, coords, z)
    return (
        layer_out,
        input_grad,
        small_grads[:n_attn],
        small_grads[2 * n_attn : 2 * n_attn + n_head],
        small_grads[2 * n_attn + n_head :],
        query_wgrad,
        key_wgrad,
        value_wgrad,
        out_wgrad,
        small_grads[n_attn : 2 * n_attn],
        gate_wgrad,
        upward_wgrad,
        down_wgrad,
    )


def normalize(values, gain):
    inverse = lax.rsqrt(jnp.mean(values * values, axis=-1, keepdims=True) + EPSILON)
    return values * inverse * gain


def rotate(values, cos_table, sine_table):
    halfway = values.shape[-1] // 2
    turned = jnp.concatenate([-values[..., halfway:], values[..., :halfway]], axis=-1)
    return values * cos_table + turned * sine_table


def placement_of(lengths, offset, total):
    places = offset + jnp.arange(total, dtype=jnp.int32)
    ends = running_ends(lengths)
    before = (ends[:, None, :] <= places[None, :, None]).astype(jnp.int32)
    document = jnp.sum(before, axis=2)
    doc_start = jnp.sum(before * lengths[:, None, :], axis=2)
    return (document, places[None, :] - doc_start, places)


def rotary_tables(position, head_size):
    frequency = jnp.exp(
        jnp.arange(head_size // 2, dtype=jnp.float32) * (-2.0 / head_size) * math.log(ROPE_BASE)
    )
    angles = position.astype(jnp.float32)[..., None] * frequency
    angles = jnp.concatenate([angles, angles], axis=-1)
    return (jnp.cos(angles)[:, :, None, :], jnp.sin(angles)[:, :, None, :])


def head_path(raw_rows, gain, cos_table, sine_table):
    shaped = raw_rows.reshape(raw_rows.shape[0], raw_rows.shape[1], -1, gain.shape[0])
    return rotate(normalize(shaped, gain), cos_table, sine_table)


def block_size(total):
    return max((divisor for divisor in range(1, min(total, 512) + 1) if total % divisor == 0))


def silu_slope(gate_proj):
    logistic = jax.nn.sigmoid(gate_proj)
    return logistic * (1.0 + gate_proj * (1.0 - logistic))


def shards(
    hidden_in,
    out_grad,
    doc_lengths,
    norm_attn,
    query_gain,
    key_gain,
    query_weight,
    key_weight,
    value_weight,
    output_weight,
    norm_mlp,
    gate_weight,
    upward_weight,
    down_weight,
):
    attn_set = (
        lax.all_gather(query_weight, ("dp", "blk", "fsdp"), axis=0, tiled=True),
        lax.all_gather(key_weight, ("dp", "blk", "fsdp"), axis=0, tiled=True),
        lax.all_gather(value_weight, ("dp", "blk", "fsdp"), axis=0, tiled=True),
        lax.all_gather(output_weight, ("dp", "blk", "fsdp"), axis=0, tiled=True),
        lax.all_gather(norm_attn, ("dp", "blk", "fsdp"), axis=0, tiled=True),
        lax.all_gather(query_gain, ("dp", "blk", "fsdp"), axis=0, tiled=True),
        lax.all_gather(key_gain, ("dp", "blk", "fsdp"), axis=0, tiled=True),
        lax.all_gather(norm_mlp, ("dp", "blk", "fsdp"), axis=0, tiled=True),
    )
    query_mat, key_mat, value_mat, out_mat = (attn_set[0], attn_set[1], attn_set[2], attn_set[3])
    gain_attn = attn_set[4].astype(jnp.float32)
    gain_query = attn_set[5].astype(jnp.float32)
    gain_key = attn_set[6].astype(jnp.float32)
    gain_mlp = attn_set[7].astype(jnp.float32)
    gate_mat, upward_mat, down_mat = (
        lax.all_gather(gate_weight, ("dp", "blk"), axis=0, tiled=True),
        lax.all_gather(upward_weight, ("dp", "blk"), axis=0, tiled=True),
        lax.all_gather(down_weight, ("dp", "blk"), axis=0, tiled=True),
    )
    seq_count, local_rows, _width = hidden_in.shape
    head_size = gain_key.shape[0]
    heads_kv = key_mat.shape[1] // head_size
    heads_q = query_mat.shape[1] // head_size
    group_size = heads_q // heads_kv
    softmax_scale = 1.0 / math.sqrt(head_size)
    offset = lax.axis_index(("blk", "fsdp")) * local_rows
    query_doc, query_pos, query_place = placement_of(doc_lengths, offset, local_rows)
    cos_table, sine_table = rotary_tables(query_pos, head_size)
    layer_in = hidden_in.astype(jnp.float32)
    first_norm = normalize(layer_in, gain_attn).astype(jnp.bfloat16)
    query_raw = jnp.dot(first_norm, query_mat, preferred_element_type=jnp.float32)
    key_raw = jnp.dot(first_norm, key_mat, preferred_element_type=jnp.float32)
    value_rows = jnp.dot(first_norm, value_mat, preferred_element_type=jnp.float32).astype(
        jnp.bfloat16
    )
    query_rows = head_path(query_raw, gain_query, cos_table, sine_table).astype(jnp.bfloat16)
    query_rows = query_rows.reshape(seq_count, local_rows, heads_kv, group_size, head_size)
    key_rows = head_path(key_raw, gain_key, cos_table, sine_table).astype(jnp.bfloat16)
    key_rows = key_rows.reshape(seq_count, local_rows, heads_kv * head_size)

    def score_block(key_part, first_key):
        key_count = key_part.shape[1]
        key_heads = key_part.reshape(seq_count, key_count, heads_kv, head_size)
        scores = (
            jnp.einsum(
                "sckgd,spkd->skgcp", query_rows, key_heads, preferred_element_type=jnp.float32
            )
            * softmax_scale
        )
        key_doc, _key_pos, key_place = placement_of(doc_lengths, first_key, key_count)
        visible = (query_doc[:, None, None, :, None] == key_doc[:, None, None, None, :]) & (
            key_place[None, None, None, None, :] <= query_place[None, None, None, :, None]
        )
        return (scores, visible)

    def attend_block(running, key_part, value_part, first_key):
        run_max, run_total, run_sum = running
        scores, visible = score_block(key_part, first_key)
        masked = jnp.where(visible, scores, MASKED)
        new_max = jnp.maximum(run_max, jnp.max(masked, axis=-1))
        weights = jnp.where(visible, jnp.exp(masked - new_max[..., None]), 0.0)
        rescale = jnp.exp(run_max - new_max)
        value_heads = value_part.reshape(seq_count, -1, heads_kv, head_size)
        update = jnp.einsum(
            "skgcp,spkd->sckgd",
            weights.astype(jnp.bfloat16),
            value_heads,
            preferred_element_type=jnp.float32,
        )
        rescale_rows = jnp.transpose(rescale, (0, 3, 1, 2))[..., None]
        return (
            new_max,
            run_total * rescale + jnp.sum(weights, axis=-1),
            run_sum * rescale_rows + update,
        )

    start_carry = (
        jnp.full((seq_count, heads_kv, group_size, local_rows), MASKED, jnp.float32),
        jnp.zeros((seq_count, heads_kv, group_size, local_rows), jnp.float32),
        jnp.zeros((seq_count, local_rows, heads_kv, group_size, head_size), jnp.float32),
    )
    first_key = jnp.int32(0)
    key_part = lax.all_gather(key_rows, ("blk", "fsdp"), axis=1, tiled=True)
    value_part = lax.all_gather(value_rows, ("blk", "fsdp"), axis=1, tiled=True)
    piece_rows = key_part.shape[1]
    fold_block_len = block_size(piece_rows)

    def one_block(block_index, inner):
        begin_row = block_index * fold_block_len
        return attend_block(
            inner,
            lax.dynamic_slice_in_dim(key_part, begin_row, fold_block_len, 1),
            lax.dynamic_slice_in_dim(value_part, begin_row, fold_block_len, 1),
            first_key + begin_row,
        )

    running = lax.fori_loop(0, piece_rows // fold_block_len, one_block, start_carry)
    run_max, run_total, run_sum = running
    attn_mix = run_sum / jnp.transpose(run_total, (0, 3, 1, 2))[..., None]
    log_total = run_max + jnp.log(run_total)
    mix_rows = attn_mix.reshape(seq_count, local_rows, heads_q * head_size).astype(jnp.bfloat16)
    residual = layer_in + jnp.dot(mix_rows, out_mat, preferred_element_type=jnp.float32)
    second_norm = normalize(residual, gain_mlp).astype(jnp.bfloat16)
    pair_rows = lax.all_gather(second_norm, "fsdp", axis=1, tiled=True)
    gate_proj = jnp.dot(pair_rows, gate_mat, preferred_element_type=jnp.float32)
    upward_proj = jnp.dot(pair_rows, upward_mat, preferred_element_type=jnp.float32)
    hidden_rows = (jax.nn.silu(gate_proj) * upward_proj).astype(jnp.bfloat16)
    down_part = jnp.einsum("scf,df->scd", hidden_rows, down_mat, preferred_element_type=jnp.float32)
    mlp_out = lax.psum_scatter(
        down_part.astype(jnp.bfloat16), "fsdp", scatter_dimension=1, tiled=True
    ).astype(jnp.float32)
    layer_out = (residual + mlp_out).astype(jnp.bfloat16)
    top_grad = out_grad.astype(jnp.float32)
    gate_back, upward_back, down_back = (
        lax.all_gather(gate_weight, ("dp", "blk"), axis=0, tiled=True),
        lax.all_gather(upward_weight, ("dp", "blk"), axis=0, tiled=True),
        lax.all_gather(down_weight, ("dp", "blk"), axis=0, tiled=True),
    )
    pair_grad = lax.all_gather(out_grad, "fsdp", axis=1, tiled=True)
    hidden_grad = jnp.einsum(
        "scd,df->scf", pair_grad, down_back, preferred_element_type=jnp.float32
    )
    down_wgrad = jnp.einsum(
        "scd,scf->df", pair_grad, hidden_rows, preferred_element_type=jnp.float32
    )
    gate_grad = (hidden_grad * upward_proj * silu_slope(gate_proj)).astype(jnp.bfloat16)
    upward_grad = (hidden_grad * jax.nn.silu(gate_proj)).astype(jnp.bfloat16)
    gate_wgrad = jnp.einsum("scd,scf->df", pair_rows, gate_grad, preferred_element_type=jnp.float32)
    upward_wgrad = jnp.einsum(
        "scd,scf->df", pair_rows, upward_grad, preferred_element_type=jnp.float32
    )
    norm_part = jnp.einsum("scf,df->scd", gate_grad, gate_back, preferred_element_type=jnp.float32)
    norm_part = norm_part + jnp.einsum(
        "scf,df->scd", upward_grad, upward_back, preferred_element_type=jnp.float32
    )
    second_grad = lax.psum_scatter(
        norm_part.astype(jnp.bfloat16), "fsdp", scatter_dimension=1, tiled=True
    ).astype(jnp.float32)
    mlp_wgrads = (
        lax.psum_scatter(gate_wgrad, ("dp", "blk"), scatter_dimension=0, tiled=True),
        lax.psum_scatter(upward_wgrad, ("dp", "blk"), scatter_dimension=0, tiled=True),
        lax.psum_scatter(down_wgrad, ("dp", "blk"), scatter_dimension=0, tiled=True),
    )
    _second_value, second_pull = jax.vjp(normalize, residual, gain_mlp)
    residual_part, gain_mlp_grad = second_pull(second_grad)
    residual_grad = top_grad + residual_part
    query_back, key_back, value_back, out_back = (
        lax.all_gather(query_weight, ("dp", "blk", "fsdp"), axis=0, tiled=True),
        lax.all_gather(key_weight, ("dp", "blk", "fsdp"), axis=0, tiled=True),
        lax.all_gather(value_weight, ("dp", "blk", "fsdp"), axis=0, tiled=True),
        lax.all_gather(output_weight, ("dp", "blk", "fsdp"), axis=0, tiled=True),
    )
    residual_low = residual_grad.astype(jnp.bfloat16)
    out_wgrad = jnp.einsum(
        "sce,scd->ed", mix_rows, residual_low, preferred_element_type=jnp.float32
    )
    mix_grad = jnp.einsum("scd,ed->sce", residual_low, out_back, preferred_element_type=jnp.float32)
    mix_grad = mix_grad.astype(jnp.bfloat16).reshape(
        seq_count, local_rows, heads_kv, group_size, head_size
    )
    delta = jnp.transpose(jnp.sum(mix_grad.astype(jnp.float32) * attn_mix, axis=-1), (0, 2, 3, 1))
    key_all, value_all = (
        lax.all_gather(key_rows, ("blk", "fsdp"), axis=1, tiled=True),
        lax.all_gather(value_rows, ("blk", "fsdp"), axis=1, tiled=True),
    )
    full_rows = key_all.shape[1]
    block_len = block_size(full_rows)

    def back_block(block_index, running_back):
        query_acc, key_buffer, value_buffer = running_back
        first_key = block_index * block_len
        key_part = lax.dynamic_slice_in_dim(key_all, first_key, block_len, 1)
        value_part = lax.dynamic_slice_in_dim(value_all, first_key, block_len, 1)
        key_heads = key_part.reshape(seq_count, block_len, heads_kv, head_size)
        value_heads = value_part.reshape(seq_count, block_len, heads_kv, head_size)
        scores, visible = score_block(key_part, first_key)
        probs = jnp.where(
            visible, jnp.exp(jnp.where(visible, scores, MASKED) - log_total[..., None]), 0.0
        )
        probs_grad = jnp.einsum(
            "sckgd,spkd->skgcp", mix_grad, value_heads, preferred_element_type=jnp.float32
        )
        score_grad = (probs * (probs_grad - delta[..., None])).astype(jnp.bfloat16)
        query_acc = (
            query_acc
            + jnp.einsum(
                "skgcp,spkd->sckgd", score_grad, key_heads, preferred_element_type=jnp.float32
            )
            * softmax_scale
        )
        key_piece = (
            jnp.einsum(
                "skgcp,sckgd->spkd", score_grad, query_rows, preferred_element_type=jnp.float32
            )
            * softmax_scale
        )
        value_piece = jnp.einsum(
            "skgcp,sckgd->spkd",
            probs.astype(jnp.bfloat16),
            mix_grad,
            preferred_element_type=jnp.float32,
        )
        key_buffer = lax.dynamic_update_slice_in_dim(
            key_buffer, key_piece.reshape(seq_count, block_len, -1), first_key, 1
        )
        value_buffer = lax.dynamic_update_slice_in_dim(
            value_buffer, value_piece.reshape(seq_count, block_len, -1), first_key, 1
        )
        return (query_acc, key_buffer, value_buffer)

    back_init = (
        jnp.zeros((seq_count, local_rows, heads_kv, group_size, head_size), jnp.float32),
        jnp.zeros((seq_count, full_rows, heads_kv * head_size), jnp.float32),
        jnp.zeros((seq_count, full_rows, heads_kv * head_size), jnp.float32),
    )
    query_acc, key_buffer, value_buffer = lax.fori_loop(
        0, full_rows // block_len, back_block, back_init
    )
    key_grad, value_grad = (
        lax.psum_scatter(
            key_buffer.astype(jnp.bfloat16), ("blk", "fsdp"), scatter_dimension=1, tiled=True
        ).astype(jnp.float32),
        lax.psum_scatter(
            value_buffer.astype(jnp.bfloat16), ("blk", "fsdp"), scatter_dimension=1, tiled=True
        ).astype(jnp.float32),
    )

    def query_path(raw_rows, gain):
        return head_path(raw_rows, gain, cos_table, sine_table)

    _query_value, query_pull = jax.vjp(query_path, query_raw, gain_query)
    query_raw_grad, gain_query_grad = query_pull(
        query_acc.reshape(seq_count, local_rows, heads_q, head_size)
    )
    _key_value, key_pull = jax.vjp(query_path, key_raw, gain_key)
    key_raw_grad, gain_key_grad = key_pull(
        key_grad.reshape(seq_count, local_rows, heads_kv, head_size)
    )
    query_low = query_raw_grad.astype(jnp.bfloat16)
    key_low = key_raw_grad.astype(jnp.bfloat16)
    value_low = value_grad.astype(jnp.bfloat16)
    query_wgrad = jnp.einsum(
        "scd,sce->de", first_norm, query_low, preferred_element_type=jnp.float32
    )
    key_wgrad = jnp.einsum("scd,sce->de", first_norm, key_low, preferred_element_type=jnp.float32)
    value_wgrad = jnp.einsum(
        "scd,sce->de", first_norm, value_low, preferred_element_type=jnp.float32
    )
    first_grad = jnp.einsum(
        "sce,de->scd", query_low, query_back, preferred_element_type=jnp.float32
    )
    first_grad = first_grad + jnp.einsum(
        "sce,de->scd", key_low, key_back, preferred_element_type=jnp.float32
    )
    first_grad = first_grad + jnp.einsum(
        "sce,de->scd", value_low, value_back, preferred_element_type=jnp.float32
    )
    _first_value, first_pull = jax.vjp(normalize, layer_in, gain_attn)
    layer_part, gain_attn_grad = first_pull(first_grad)
    input_grad = residual_grad + layer_part
    attn_wgrads = (
        lax.psum_scatter(query_wgrad, ("dp", "blk", "fsdp"), scatter_dimension=0, tiled=True),
        lax.psum_scatter(key_wgrad, ("dp", "blk", "fsdp"), scatter_dimension=0, tiled=True),
        lax.psum_scatter(value_wgrad, ("dp", "blk", "fsdp"), scatter_dimension=0, tiled=True),
        lax.psum_scatter(out_wgrad, ("dp", "blk", "fsdp"), scatter_dimension=0, tiled=True),
        lax.psum_scatter(gain_attn_grad, ("dp", "blk", "fsdp"), scatter_dimension=0, tiled=True),
        lax.psum_scatter(gain_query_grad, ("dp", "blk", "fsdp"), scatter_dimension=0, tiled=True),
        lax.psum_scatter(gain_key_grad, ("dp", "blk", "fsdp"), scatter_dimension=0, tiled=True),
        lax.psum_scatter(gain_mlp_grad, ("dp", "blk", "fsdp"), scatter_dimension=0, tiled=True),
    )
    return (
        layer_out,
        input_grad,
        attn_wgrads[4],
        attn_wgrads[5],
        attn_wgrads[6],
        attn_wgrads[0],
        attn_wgrads[1],
        attn_wgrads[2],
        attn_wgrads[3],
        attn_wgrads[7],
        mlp_wgrads[0],
        mlp_wgrads[1],
        mlp_wgrads[2],
    )


def solution(mesh):
    sizes = dict(mesh.shape)
    layered = (sizes["dp"], sizes["blk"], sizes["fsdp"]) == (4, 4, 2)
    return jax.shard_map(
        layer_shards if layered else shards,
        mesh=mesh,
        in_specs=(
            P("dp", ("blk", "fsdp"), None),
            P("dp", ("blk", "fsdp"), None),
            P("dp", None),
            P(("dp", "blk", "fsdp")),
            P(("dp", "blk", "fsdp")),
            P(("dp", "blk", "fsdp")),
            P(("dp", "blk", "fsdp"), None),
            P(("dp", "blk", "fsdp"), None),
            P(("dp", "blk", "fsdp"), None),
            P(("dp", "blk", "fsdp"), None),
            P(("dp", "blk", "fsdp")),
            P(("dp", "blk"), "fsdp"),
            P(("dp", "blk"), "fsdp"),
            P(("dp", "blk"), "fsdp"),
        ),
        out_specs=(
            P("dp", ("blk", "fsdp"), None),
            P("dp", ("blk", "fsdp"), None),
            P(("dp", "blk", "fsdp")),
            P(("dp", "blk", "fsdp")),
            P(("dp", "blk", "fsdp")),
            P(("dp", "blk", "fsdp"), None),
            P(("dp", "blk", "fsdp"), None),
            P(("dp", "blk", "fsdp"), None),
            P(("dp", "blk", "fsdp"), None),
            P(("dp", "blk", "fsdp")),
            P(("dp", "blk"), "fsdp"),
            P(("dp", "blk"), "fsdp"),
            P(("dp", "blk"), "fsdp"),
        ),
        check_vma=False,
    )
```

```python
import functools
import math

import jax
import jax.numpy as jnp
from jax import lax
from jax.experimental import pallas as pl
from jax.experimental.pallas import tpu as pltpu
from jax.sharding import PartitionSpec as P

EPSILON = 1e-06
ROPE_BASE = 1000000.0
MASKED = -1e30
BF = jnp.bfloat16
F32 = jnp.float32
EVERY = ("dp", "blk", "fsdp")


def running_ends(lengths):
    parts = [lengths[..., :1]]
    for index in range(1, lengths.shape[-1]):
        parts.append(parts[-1] + lengths[..., index : index + 1])
    return jnp.concatenate(parts, axis=-1)


SWAP_X = [(0, 2), (2, 0), (1, 3), (3, 1)]
SWAP_C = [(0, 1), (1, 0), (2, 3), (3, 2)]
SWAP_Y = [(0, 1), (1, 0)]
BLOCK = 128
PIECES = 8


def over_x(value):
    return lax.ppermute(value, "dp", SWAP_X)


def over_c(value):
    return lax.ppermute(value, "dp", SWAP_C)


def over_y(value):
    return lax.ppermute(value, "fsdp", SWAP_Y)


def after(value, *before):
    return lax.optimization_barrier((value, *before))[0]


def sum_low(*parts):
    return functools.reduce(lambda a, b: a + b, [p.astype(F32) for p in parts]).astype(BF)


def by_bit(bit, zero, one):
    return jnp.where(bit == 1, one, zero)


def pick(value, index, axis):
    return lax.dynamic_index_in_dim(value, index, axis, keepdims=False)


def flip_where(bit, value, axis):
    first, second = jnp.split(value, 2, axis)
    return jnp.where(bit == 1, jnp.concatenate([second, first], axis), value)


def together(*values):
    return lax.optimization_barrier(values)


def layer_gather(low, high, core_after=()):
    low_x, high_y = together(over_x(low), over_y(high))
    low_row, high_row = together(jnp.concatenate([low, low_x]), jnp.concatenate([high, high_y]))
    low_both, high_both = together(over_y(low_row), over_x(high_row))
    near = [low_row, low_both, high_row, high_both]
    last = [after(piece, *core_after) if core_after else piece for piece in (low_both, high_both)]
    sent = [low_row, last[0], high_row, last[1]]
    return near + [over_c(piece) for piece in sent]


def scatter_start(product, core_after=(), middle=None):
    sent_low, sent_high = product(1024, 1536), product(1536, 2048)
    more = middle((sent_low[0], sent_high[0])) if middle else ()
    here = product(0, 1024, sent_low[0], sent_high[0], *more)
    far_low, far_high = together(
        over_c(after(sent_low[0], *core_after)), over_c(after(sent_high[0], *core_after))
    )
    second = together(
        sum_low(*[part[256:512] for part in here], far_low[256:]),
        sum_low(*[part[768:] for part in here], far_high[256:]),
    )
    low_back, high_back = together(over_y(second[0]), over_x(second[1]))
    return here, (far_low, far_high), second, (low_back, high_back)


def scatter_end(state, before=()):
    here, (far_low, far_high), _, (low_back, high_back) = state
    if before:
        low_back, high_back, *_ = together(low_back, high_back, *before)
    third = together(
        sum_low(*[part[128:256] for part in here], far_low[128:256], low_back[128:]),
        sum_low(*[part[640:768] for part in here], far_high[128:256], high_back[128:]),
    )
    low_last, high_last = together(over_x(third[0]), over_y(third[1]))
    parts = (
        (*[part[:128] for part in here], far_low[:128], low_back[:128], low_last),
        (*[part[512:640] for part in here], far_high[:128], high_back[:128], high_last),
    )
    return parts, third


def product_of(rows, matrix, dims, more=None):
    def product(first, last, *before):
        part = rows[first:last]
        part = after(part, *before) if before else part
        out = lax.dot_general(part, matrix, dims, preferred_element_type=F32)
        if more is None or first == 0:
            return [out.astype(BF)] + (more[first] if more else [])
        return [(out + more[first][0].astype(F32)).astype(BF)]

    return product


def total_of(parts):
    return functools.reduce(lambda a, b: a + b, [p.astype(F32) for p in parts])


def blk_gather(own):
    return lax.all_gather(own, "blk", axis=0, tiled=True)


def blk_scatter(partial):
    return lax.psum_scatter(partial, "blk", scatter_dimension=0, tiled=True)


def swap_z(value, step):
    return lax.ppermute(value, "blk", [(z, z ^ step) for z in range(4)])


def small_gather(value, coords, z):
    x_bit, c_bit, y_bit = coords
    for bit, move in (
        (y_bit, over_y),
        (c_bit, over_c),
        (x_bit, over_x),
        (z % 2, functools.partial(swap_z, step=1)),
        (z // 2, functools.partial(swap_z, step=2)),
    ):
        got = move(value)
        value = flip_where(bit, jnp.stack([value, got]), 0)
    return value.reshape(4, 2, 2, 2, -1), got


def small_scatter(value, coords, z, before):
    x_bit, c_bit, y_bit = coords
    value = value.reshape(2, 2, 2, 2, 2, -1)
    for bit, move, axis in ((x_bit, over_x, 0), (c_bit, over_c, 0), (y_bit, over_y, 2)):
        value = pick(value, bit, axis) + move(pick(value, 1 - bit, axis))
    value = after(value, *before)
    for bit, step in ((z // 2, 2), (z % 2, 1)):
        value = pick(value, bit, 0) + swap_z(pick(value, 1 - bit, 0), step)
    return value


def width_blocks(value):
    step = value.shape[-1] // 16
    return [value[..., i * step : (i + 1) * step] for i in range(16)]


def model_order(value):
    blocks = width_blocks(value)
    return jnp.concatenate([blocks[j * 4 + i] for i in range(4) for j in range(4)], axis=-1)


def trade(value, bit, move, axis):
    keep, got = pick(value, bit, axis), move(pick(value, 1 - bit, axis))
    return by_bit(bit, jnp.stack([keep, got], axis), jnp.stack([got, keep], axis))


def join(keep, got, bit, axis):
    return by_bit(bit, jnp.stack([keep, got], axis), jnp.stack([got, keep], axis))


def row_moves():
    first, second = [], []
    for d in range(4):
        for z in range(4):
            for y in range(2):
                source = d * 8 + z * 2 + y
                target = (d // 2) * 2 + z // 2
                first.append((source, target * 8 + (2 * (d % 2) + z % 2) * 2 + y))
                second.append((source, target * 8 + (2 * (d % 2) + 1 - z % 2) * 2 + y))
    return first, second


def sort_width(read, write, width):
    step = width // 16
    for i in range(4):
        for j in range(4):
            write(slice((i * 4 + j) * step, (i * 4 + j + 1) * step), read(slice((j * 4 + i) * step, (j * 4 + i + 1) * step)))


def send_rows_kernel(odd_ref, value_ref, first_ref, second_ref):
    odd = odd_ref[0]
    for out, at in ((first_ref, odd), (second_ref, 1 - odd)):

        def write(cols, value, out=out):
            out[:, cols] = value

        sort_width(lambda cols, at=at: value_ref[at, :, cols], write, out.shape[1])


def send_rows(value, odd):
    shape = jax.ShapeDtypeStruct(value.shape[1:], value.dtype)
    return pl.pallas_call(
        send_rows_kernel,
        in_specs=[pl.BlockSpec(memory_space=pltpu.SMEM), pl.BlockSpec(memory_space=pltpu.VMEM)],
        out_specs=[pl.BlockSpec(memory_space=pltpu.VMEM)] * 2,
        out_shape=[shape, shape],
    )(odd.reshape(1), value)


def keep_rows_kernel(odd_ref, first_ref, second_ref, out_ref):
    odd = odd_ref[0]
    for got, at in ((first_ref, odd), (second_ref, 1 - odd)):

        def write(cols, value, at=at):
            out_ref[at, :, cols] = value.astype(out_ref.dtype)

        sort_width(lambda cols, got=got: got[:, cols], write, got.shape[1])


def keep_rows(first, second, odd, dtype):
    return pl.pallas_call(
        keep_rows_kernel,
        in_specs=[pl.BlockSpec(memory_space=pltpu.SMEM)] + [pl.BlockSpec(memory_space=pltpu.VMEM)] * 2,
        out_specs=pl.BlockSpec(memory_space=pltpu.VMEM),
        out_shape=jax.ShapeDtypeStruct((2, *first.shape), dtype),
    )(odd.reshape(1), first, second)


def sort_kernel(value_ref, out_ref):
    def write(cols, value):
        out_ref[:, cols] = value.astype(out_ref.dtype)

    sort_width(lambda cols: value_ref[:, cols], write, value_ref.shape[1])


def sort_model(value, dtype):
    return pl.pallas_call(
        sort_kernel,
        in_specs=[pl.BlockSpec(memory_space=pltpu.VMEM)],
        out_specs=pl.BlockSpec(memory_space=pltpu.VMEM),
        out_shape=jax.ShapeDtypeStruct(value.shape, dtype),
    )(value)


def rows_in(sent, odd):
    moves = row_moves()
    got_first = lax.ppermute(sent[0], EVERY, moves[0])
    got_second = lax.ppermute(sent[1], EVERY, moves[1])
    return by_bit(odd, got_first, got_second), by_bit(odd, got_second, got_first)


def rows_back(sent):
    moves = row_moves()
    return [lax.ppermute(s, EVERY, [(b, a) for a, b in m]) for s, m in zip(sent, moves, strict=True)]


def rows_out(low, high, odd):
    return rows_back((by_bit(odd, low, high), by_bit(odd, high, low)))


def block_rows(scalars, row, block):
    c_bit, y_bit = scalars[0], scalars[1]
    far_c = jnp.where(c_bit == (block >> 2), 0, 1)
    far_y = jnp.where(y_bit == (block & 1), 0, 1)
    if (block >> 1) & 1:
        at = far_c * 8 + 4 + row * 2 + far_y
    else:
        at = far_c * 8 + far_y * 2 + row
    return pl.ds(pl.multiple_of(at * BLOCK, BLOCK), BLOCK)


def swap_halves(value):
    return pltpu.roll(value, value.shape[-1] // 2, 1)


def head_forward(raw, gain, cos, sine):
    inverse = lax.rsqrt(jnp.mean(raw * raw, axis=-1, keepdims=True) + EPSILON)
    scaled = raw * inverse * gain
    return scaled * cos + swap_halves(scaled) * sine


def head_backward(grad, raw, gain, cos, sine):
    inverse = lax.rsqrt(jnp.mean(raw * raw, axis=-1, keepdims=True) + EPSILON)
    unit = raw * inverse
    back = grad * cos + swap_halves(grad * sine)
    gain_grad = jnp.sum(back * unit, axis=0, keepdims=True)
    scaled = back * gain
    return inverse * (scaled - unit * jnp.mean(scaled * unit, axis=-1, keepdims=True)), gain_grad


def visible_pairs(scalars, row, first_query, queries, keys, docs):
    place = first_query + lax.broadcasted_iota(jnp.int32, (queries, 1), 0)
    start = jnp.zeros_like(place)
    for doc in range(docs - 1):
        end = scalars[2 + row * docs + doc]
        start = jnp.where(place >= end, end, start)
    key_place = lax.broadcasted_iota(jnp.int32, (queries, keys), 1)
    return (key_place >= start) & (key_place <= place)


def fetch(pieces, held, sems, base=0):
    size = held.shape[0] // len(pieces)
    return [
        pltpu.make_async_copy(piece, held.at[pl.ds(i * size, size), :], sems.at[base + i])
        for i, piece in enumerate(pieces)
    ]


def load_row(scalars, row, raw_ref, cos_ref, sine_ref, gain_ref, q_s, k_s, v_s, groups, blocks):
    width = 128
    for block in range(blocks):
        rel = block_rows(scalars, row, block)
        rows = slice(block * BLOCK, block * BLOCK + BLOCK)
        cos, sine = cos_ref[0, rows, :], sine_ref[0, rows, :]
        for g in range(groups):
            raw = raw_ref[rel, g * width : (g + 1) * width]
            q_s[rows, g * width : (g + 1) * width] = head_forward(
                raw, gain_ref[0:1, :], cos, sine
            ).astype(BF)
        raw = raw_ref[rel, groups * width : (groups + 1) * width]
        k_s[rows, :] = head_forward(raw, gain_ref[1:2, :], cos, sine).astype(BF)
        v_s[rows, :] = raw_ref[rel, (groups + 1) * width : (groups + 2) * width].astype(BF)


ROWS_C = (((1,), (1,)), ((), ()))
COLS_C = (((0,), (0,)), ((), ()))


def attend_kernel(scalars, cos_ref, sine_ref, gain_ref, *refs, groups, docs, step):
    raw_s, mix_ref, q_s, k_s, v_s = refs
    row = pl.program_id(0)
    total = k_s.shape[0]
    load_row(scalars, row, raw_s, cos_ref, sine_ref, gain_ref, q_s, k_s, v_s, groups, total // BLOCK)
    scale = 1.0 / math.sqrt(128)
    for first in range(0, total, step):
        keys = first + step
        visible = visible_pairs(scalars, row, first, step, keys, docs)
        for g in range(groups):
            query = q_s[first : first + step, g * 128 : (g + 1) * 128]
            scores = lax.dot_general(query, k_s[:keys, :], ROWS_C, preferred_element_type=F32) * scale
            scores = jnp.where(visible, scores, MASKED)
            weights = jnp.exp(scores - jnp.max(scores, axis=-1, keepdims=True))
            norm = jnp.sum(weights, axis=-1, keepdims=True)
            mixed = jnp.dot(weights.astype(BF), v_s[:keys, :], preferred_element_type=F32) / norm
            for part in range(step // BLOCK):
                rel = block_rows(scalars, row, first // BLOCK + part)
                mix_ref[rel, g * 128 : (g + 1) * 128] = mixed[part * BLOCK : (part + 1) * BLOCK].astype(BF)


def attend_back_kernel(scalars, cos_ref, sine_ref, gain_ref, *refs, groups, docs, step):
    raw_s, dmix_s, draw_ref, dgain_ref, q_s, k_s, v_s, dk_s, dv_s = refs
    row = pl.program_id(0)
    total = k_s.shape[0]
    load_row(scalars, row, raw_s, cos_ref, sine_ref, gain_ref, q_s, k_s, v_s, groups, total // BLOCK)
    scale = 1.0 / math.sqrt(128)
    dk_s[...] = jnp.zeros_like(dk_s)
    dv_s[...] = jnp.zeros_like(dv_s)
    query_gain = jnp.zeros((1, 128), F32)
    for first in range(0, total, step):
        keys = first + step
        visible = visible_pairs(scalars, row, first, step, keys, docs)
        order = [block_rows(scalars, row, first // BLOCK + part) for part in range(step // BLOCK)]
        for g in range(groups):
            cols = slice(g * 128, (g + 1) * 128)
            query = q_s[first : first + step, cols]
            dmix = jnp.concatenate([dmix_s[rel, cols] for rel in order], axis=0)
            scores = lax.dot_general(query, k_s[:keys, :], ROWS_C, preferred_element_type=F32) * scale
            scores = jnp.where(visible, scores, MASKED)
            weights = jnp.exp(scores - jnp.max(scores, axis=-1, keepdims=True))
            probs = weights / jnp.sum(weights, axis=-1, keepdims=True)
            dprobs = lax.dot_general(dmix, v_s[:keys, :], ROWS_C, preferred_element_type=F32)
            delta = jnp.sum(probs * dprobs, axis=-1, keepdims=True)
            dscores = (probs * (dprobs - delta)).astype(BF)
            dquery = jnp.dot(dscores, k_s[:keys, :], preferred_element_type=F32) * scale
            dk_s[:keys, :] += lax.dot_general(dscores, query, COLS_C, preferred_element_type=F32)
            dv_s[:keys, :] += lax.dot_general(probs.astype(BF), dmix, COLS_C, preferred_element_type=F32)
            for part, rel in enumerate(order):
                rows = slice(first + part * BLOCK, first + (part + 1) * BLOCK)
                draw, gain_part = head_backward(
                    dquery[part * BLOCK : (part + 1) * BLOCK], raw_s[rel, cols], gain_ref[0:1, :],
                    cos_ref[0, rows, :], sine_ref[0, rows, :],
                )
                draw_ref[rel, cols] = draw.astype(BF)
                query_gain += gain_part
    key_gain = jnp.zeros((1, 128), F32)
    cols = slice(groups * 128, (groups + 1) * 128)
    for block in range(total // BLOCK):
        rel = block_rows(scalars, row, block)
        rows = slice(block * BLOCK, (block + 1) * BLOCK)
        draw, gain_part = head_backward(
            dk_s[rows, :] * scale, raw_s[rel, cols], gain_ref[1:2, :], cos_ref[0, rows, :], sine_ref[0, rows, :]
        )
        draw_ref[rel, cols] = draw.astype(BF)
        draw_ref[rel, (groups + 1) * 128 : (groups + 2) * 128] = dv_s[rows, :].astype(BF)
        key_gain += gain_part
    dgain_ref[0, :, :] = jnp.concatenate([query_gain, key_gain, jnp.zeros((6, 128), F32)], axis=0)


ATTEND_STEP = 256


def attend(scalars, raw, cos, sine, gains, groups, docs, dmix=None):
    total, width = cos.shape[1], raw.shape[1]
    by_row = pl.BlockSpec((1, total, 128), lambda r, s: (r, 0, 0))
    back = dmix is not None
    given = [raw, dmix] if back else [raw]
    once = lambda columns: pl.BlockSpec((2 * total, columns), lambda r, s: (0, 0))
    out_specs = [once(width if back else groups * 128)]
    out_shape = [jax.ShapeDtypeStruct((2 * total, width if back else groups * 128), BF)]
    if back:
        out_specs.append(pl.BlockSpec((1, 8, 128), lambda r, s: (r, 0, 0)))
        out_shape.append(jax.ShapeDtypeStruct((2, 8, 128), F32))
    scratch = [
        pltpu.VMEM((total, groups * 128), BF),
        pltpu.VMEM((total, 128), BF),
        pltpu.VMEM((total, 128), BF),
    ]
    if back:
        scratch += [pltpu.VMEM((total, 128), F32), pltpu.VMEM((total, 128), F32)]
    return pl.pallas_call(
        functools.partial(
            attend_back_kernel if back else attend_kernel, groups=groups, docs=docs, step=ATTEND_STEP
        ),
        grid_spec=pltpu.PrefetchScalarGridSpec(
            num_scalar_prefetch=1,
            grid=(2,),
            in_specs=[by_row, by_row, pl.BlockSpec((8, 128), lambda r, s: (0, 0))]
            + [once(part.shape[1]) for part in given],
            out_specs=out_specs,
            scratch_shapes=scratch,
        ),
        out_shape=out_shape,
        compiler_params=pltpu.CompilerParams(vmem_limit_bytes=40 * 2**20),
        cost_estimate=pl.CostEstimate(
            flops=groups * total * total * 128 * 2 * (5 if back else 2) * 2 * 5 // 8,
            bytes_accessed=(40 if back else 12) * 2**20,
            transcendentals=groups * total * total * 2,
        ),
    )(scalars, cos, sine, gains, *given)


def pieces_kernel(matrix_ref, *refs, dims):
    pieces, (out_ref, whole_ref, held, sems, out_sem) = refs[:PIECES], refs[PIECES:]
    copies = fetch(pieces, held, sems)
    for copy in copies:
        copy.start()
    size = held.shape[0] // PIECES
    for at, copy in enumerate(copies):
        copy.wait()
        rows = slice(at * size, (at + 1) * size)
        out_ref[rows, :] = lax.dot_general(
            held[rows, :], matrix_ref[...], dims, preferred_element_type=F32
        ).astype(out_ref.dtype)
    out = pltpu.make_async_copy(held, whole_ref, out_sem)
    out.start()
    out.wait()


def pieces_dot(pieces, matrix, dims, dtype):
    rows, width = pieces[0].shape
    columns = matrix.shape[1 - dims[0][1][0]]
    vmem, anywhere = pl.BlockSpec(memory_space=pltpu.VMEM), pl.BlockSpec(memory_space=pl.ANY)
    return pl.pallas_call(
        functools.partial(pieces_kernel, dims=dims),
        in_specs=[vmem] + [anywhere] * PIECES,
        out_specs=[vmem, anywhere],
        out_shape=[
            jax.ShapeDtypeStruct((PIECES * rows, columns), dtype),
            jax.ShapeDtypeStruct((PIECES * rows, width), BF),
        ],
        scratch_shapes=[
            pltpu.VMEM((PIECES * rows, width), BF),
            pltpu.SemaphoreType.DMA((PIECES,)),
            pltpu.SemaphoreType.DMA,
        ],
        compiler_params=pltpu.CompilerParams(vmem_limit_bytes=32 * 2**20),
        cost_estimate=pl.CostEstimate(
            flops=2 * PIECES * rows * width * columns,
            bytes_accessed=4 * PIECES * rows * width + 4 * PIECES * rows * columns,
            transcendentals=0,
        ),
    )(matrix, *pieces)


UNIT_TILE = 256
TOKEN_TILE = 512


def units_kernel(both_ref, down_ref, *refs, given):
    normed, tops = refs[:given], refs[given : 2 * given]
    hidden_ref, dboth_ref = refs[2 * given : 2 * given + 2]
    *wholes, normed_s, top_s, sems, out_sems = refs[2 * given + 2 :]
    at = pl.program_id(0)
    last = pl.num_programs(0) - 1
    size = normed_s.shape[0] // PIECES
    if given == 1:
        normed, tops = ([r[0].at[pl.ds(i * size, size), :] for i in range(PIECES)] for r in (normed, tops))
    copies = fetch(normed, normed_s, sems), fetch(tops, top_s, sems, PIECES)
    outs = [
        pltpu.make_async_copy(held, whole, out_sems.at[i])
        for i, (held, whole) in enumerate(zip((normed_s, top_s), wholes))
    ]

    @pl.when(at == 0)
    def _():
        for one, other in zip(*copies, strict=True):
            one.start()
            other.start()

    per = TOKEN_TILE // size
    for tile in range(normed_s.shape[0] // TOKEN_TILE):

        @pl.when(at == 0)
        def _(tile=tile):
            for piece in range(tile * per, (tile + 1) * per):
                copies[0][piece].wait()
                copies[1][piece].wait()

        rows = slice(tile * TOKEN_TILE, (tile + 1) * TOKEN_TILE)
        both = jnp.dot(normed_s[rows, :], both_ref[...], preferred_element_type=F32)
        gate, upward = both[:, :UNIT_TILE], both[:, UNIT_TILE:]
        dhidden = jnp.dot(top_s[rows, :], down_ref[...], preferred_element_type=F32)
        logistic = 1.0 / (1.0 + jnp.exp(-gate))
        swish = gate * logistic
        hidden_ref[rows, :] = (swish * upward).astype(BF)
        dgate = dhidden * upward * (logistic * (1.0 + gate * (1.0 - logistic)))
        dboth_ref[rows, :UNIT_TILE] = dgate.astype(BF)
        dboth_ref[rows, UNIT_TILE:] = (dhidden * swish).astype(BF)

    if outs:

        @pl.when(at == 0)
        def _():
            for out in outs:
                out.start()

        @pl.when(at == last)
        def _():
            for out in outs:
                out.wait()


def units_pass(normed, tops, mat):
    given = len(normed)
    width, units = mat.shape[0], mat.shape[1] // 3
    tiles = units // UNIT_TILE
    tokens = given * normed[0].shape[0]
    anywhere = pl.BlockSpec(memory_space=pl.ANY)
    whole = jax.ShapeDtypeStruct((tokens, width), BF)
    wholes = 0 if given == 1 else 2
    return pl.pallas_call(
        functools.partial(units_kernel, given=given),
        grid=(tiles,),
        in_specs=[
            pl.BlockSpec((width, 2 * UNIT_TILE), lambda i: (0, i)),
            pl.BlockSpec((width, UNIT_TILE), lambda i: (0, 2 * tiles + i)),
        ]
        + [anywhere] * (2 * given),
        out_specs=[
            pl.BlockSpec((tokens, UNIT_TILE), lambda i: (0, i)),
            pl.BlockSpec((tokens, 2 * UNIT_TILE), lambda i: (0, i)),
        ]
        + [anywhere] * wholes,
        out_shape=[
            jax.ShapeDtypeStruct((tokens, units), BF),
            jax.ShapeDtypeStruct((tokens, 2 * units), BF),
        ]
        + [whole] * wholes,
        scratch_shapes=[
            pltpu.VMEM((tokens, width), BF),
            pltpu.VMEM((tokens, width), BF),
            pltpu.SemaphoreType.DMA((2 * PIECES,)),
            pltpu.SemaphoreType.DMA((2,)),
        ],
        compiler_params=pltpu.CompilerParams(vmem_limit_bytes=48 * 2**20),
        cost_estimate=pl.CostEstimate(
            flops=2 * tokens * width * units * 3,
            bytes_accessed=4 * tokens * width * 2 + 6 * width * units + 6 * tokens * units,
            transcendentals=tokens * units,
        ),
    )(mat, mat, *normed, *tops)


def norm_inverse(values):
    return lax.rsqrt(jnp.mean(values * values, axis=-1, keepdims=True) + EPSILON)


def norm_back(grad, unit, inverse, gain):
    scaled = grad * gain
    return inverse * (scaled - unit * jnp.mean(scaled * unit, axis=-1, keepdims=True))


def wgrad(rows, columns):
    return lax.dot_general(rows, columns, COLS_C, preferred_element_type=F32).astype(BF)


def scaled_wgrad(rows, columns, gain):
    out = lax.dot_general(rows, columns, COLS_C, preferred_element_type=F32)
    return (out * gain[:, None]).astype(BF)


CHUNKS = ((0, 3),)


def layer_shards(
    hidden_in, out_grad, doc_lengths, norm_attn, query_gain, key_gain, query_weight, key_weight,
    value_weight, output_weight, norm_mlp, gate_weight, upward_weight, down_weight,
):
    d, z, y = lax.axis_index("dp"), lax.axis_index("blk"), lax.axis_index("fsdp")
    x_bit, c_bit, odd = d // 2, d % 2, z % 2
    coords = (x_bit, c_bit, y)
    width = hidden_in.shape[-1]
    docs = doc_lengths.shape[1]
    head = query_gain.shape[0] * 32
    groups = query_weight.shape[1] // key_weight.shape[1]
    total = hidden_in.shape[1] * 8
    hidden_units = gate_weight.shape[1]
    share = width // 32
    transposed = (((1,), (1,)), ((), ()))
    plain = (((1,), (0,)), ((), ()))

    sent = *send_rows(hidden_in, odd), *send_rows(out_grad, odd)
    small = jnp.concatenate(
        [v.astype(F32) for v in (norm_attn, norm_mlp, query_gain, key_gain)]
        + [after(doc_lengths, *sent).astype(F32).reshape(-1)]
    )
    tokens, top_own = rows_in(sent[:2], odd), rows_in(sent[2:], odd)
    small_all, small_last = small_gather(small, coords, z)

    pieces = jnp.concatenate(
        [w.reshape(share, 8, -1) for w in (after(query_weight, *sent), key_weight, value_weight)], axis=-1
    )
    pieces = jnp.transpose(pieces, (1, 0, 2)).reshape(2, 2, 2, share, -1)
    pieces = trade(pieces, x_bit, over_x, 0)
    pieces = trade(pieces, y, over_y, 2)
    qkv_own = trade(pieces, c_bit, over_c, 1)

    n_attn, n_head = norm_attn.shape[0], query_gain.shape[0]
    by_device = jnp.transpose(small_all, (1, 2, 0, 3, 4)).reshape(32, -1)
    by_blk = small_all.reshape(32, -1)
    gain_attn = by_blk[:, :n_attn].reshape(-1)
    gain_mlp = by_blk[:, n_attn : 2 * n_attn].reshape(-1)
    gain_query = by_device[:, 2 * n_attn : 2 * n_attn + n_head].reshape(-1)
    gain_key = by_device[:, 2 * n_attn + n_head : 2 * n_attn + 2 * n_head].reshape(-1)
    lengths = by_device[::8, 2 * n_attn + 2 * n_head :].astype(jnp.int32).reshape(4, 2, docs)
    ends_all = running_ends(lengths)
    ends = jnp.stack(
        [ends_all[(x_bit ^ dx) * 2 + z // 2, odd] for dx in range(2)]
    )
    place = jnp.arange(total, dtype=jnp.int32)
    start = jnp.zeros((2, total), jnp.int32)
    for doc in range(docs - 1):
        start = jnp.where(place[None] >= ends[:, doc : doc + 1], ends[:, doc : doc + 1], start)
    frequency = jnp.exp(
        jnp.arange(head // 2, dtype=F32) * (-2.0 / head) * math.log(ROPE_BASE)
    )
    angles = (place[None] - start).astype(F32)[..., None] * frequency
    cos_half, sine_half = jnp.cos(angles), jnp.sin(angles)
    cos_table = jnp.concatenate([cos_half, cos_half], axis=-1)
    sine_table = jnp.concatenate([-sine_half, sine_half], axis=-1)
    scalars = jnp.concatenate([jnp.stack([c_bit, y]), ends.reshape(-1)]).astype(jnp.int32)
    head_gains = jnp.concatenate(
        [gain_query[None], gain_key[None], jnp.zeros((6, head), F32)], axis=0
    )

    quarter = hidden_units // 4
    by_quarter = [w.reshape(-1, 4, quarter // UNIT_TILE, UNIT_TILE) for w in (gate_weight, upward_weight, down_weight)]
    weight_pieces = []
    for first, last in CHUNKS:
        gates, upwards, downs = (w[:, :, first:last] for w in by_quarter)
        piece = jnp.concatenate(
            [jnp.stack([gates, upwards], axis=3).reshape(*gates.shape[:2], -1), downs.reshape(*gates.shape[:2], -1)],
            axis=-1,
        )
        weight_pieces.append(jnp.transpose(piece, (1, 0, 2)).reshape(2, 2, piece.shape[0], -1))

    def layer_weights(piece, *before):
        half = over_x(after(pick(piece, 1 - x_bit, 0), *before))
        half = join(pick(piece, x_bit, 0), half, x_bit, 0)
        return trade(half, c_bit, over_c, 1).reshape(width // 4, -1)

    owns = [layer_weights(weight_pieces[0], qkv_own)]
    arrived = tokens
    tokens = [after(t, qkv_own, *top_own, *owns) for t in tokens]
    attn_own = jnp.concatenate([qkv_own.reshape(8 * share, -1), output_weight.reshape(4 * share, -1)])
    attn_all = blk_gather(after(attn_own, small_last, *arrived, *top_own)).reshape(4, 12 * share, -1)

    layer_in = [t.astype(F32) for t in tokens]
    inverse_attn = [norm_inverse(t) for t in layer_in]
    unit_attn = [t * i for t, i in zip(layer_in, inverse_attn, strict=True)]
    units1 = layer_gather(*[u.astype(BF) for u in unit_attn], (cos_table, sine_table))
    owns += [layer_weights(piece, units1[1], units1[3]) for piece in weight_pieces[1:]]
    mats = [blk_gather(after(own, *arrived, *top_own)) for own in owns]
    tops = layer_gather(*[after(t, units1[1], units1[3]) for t in top_own])
    qkv_mat = attn_all[:, : 8 * share].reshape(width, -1)
    scaled_mat = (qkv_mat.astype(F32) * gain_attn[:, None]).astype(BF)
    raw, units1_all = pieces_dot(units1, scaled_mat, plain, F32)
    out_all = after(attn_all, raw)[:, 8 * share :].reshape(2, 2, share, width)
    out_all = trade(out_all, y, over_y, 0)
    out_mat = sort_model(jnp.swapaxes(out_all, 0, 1).reshape(-1, width), BF)
    (mix,) = attend(scalars, raw, cos_table, sine_table, head_gains, groups, docs)
    mix = after(mix, tops[1], tops[3])
    mixed, _ = scatter_end(scatter_start(product_of(mix, out_mat, plain)))
    residual = [t + total_of(parts) for t, parts in zip(layer_in, mixed, strict=True)]
    inverse_mlp = [norm_inverse(t) for t in residual]
    unit_mlp = [t * i for t, i in zip(residual, inverse_mlp, strict=True)]
    normed2 = layer_gather(*[after((u * gain_mlp).astype(BF), *tops) for u in unit_mlp])

    hiddens, dboths, boths, downs, down_wgrads, both_wgrads = [], [], [], [], [], []
    dnormed2_part = mlp_part = None
    normed2_all = top_all = None
    for (first, last), mat in zip(CHUNKS, mats, strict=True):
        units = (last - first) * UNIT_TILE
        boths.append(mat[:, : 2 * units])
        downs.append(mat[:, 2 * units :])
        if normed2_all is None:
            hidden, dboth, normed2_all, top_all = units_pass(normed2, tops, mat)
        else:
            normed2_all = after(
                normed2_all, *down_wgrads, *both_wgrads, *(part[0] for part in dnormed2_part.values())
            )
            hidden, dboth = units_pass([normed2_all], [top_all], mat)
        hiddens.append(hidden)
        dboths.append(dboth)
        if last != CHUNKS[-1][1]:
            both_wgrads.append(wgrad(normed2_all, dboth))
            down_wgrads.append(wgrad(top_all, after(hidden, both_wgrads[-1])))
            part = product_of(after(dboth, down_wgrads[-1]), boths[-1], transposed, dnormed2_part)
            dnormed2_part = {1024: part(1024, 1536), 1536: part(1536, 2048), 0: part(0, 1024)}
    down_wgrads.append(wgrad(top_all, hiddens[-1]))
    state = scatter_start(
        product_of(after(dboths[-1], down_wgrads[-1]), boths[-1], transposed, dnormed2_part)
    )
    here, _, second, _ = state
    both_wgrads.append(wgrad(after(normed2_all, *second), dboths[-1]))
    dnormed2, third = scatter_end(state, both_wgrads[-1:])
    dnormed2 = [total_of(parts) for parts in dnormed2]

    gain_mlp_grad = sum(jnp.sum(g * u, axis=0) for g, u in zip(dnormed2, unit_mlp, strict=True))
    dresidual = [
        t.astype(F32) + norm_back(g, u, i, gain_mlp)
        for t, g, u, i in zip(top_own, dnormed2, unit_mlp, inverse_mlp, strict=True)
    ]
    both_last, down_last = both_wgrads[-1], down_wgrads[-1]
    both_wgrads = [blk_scatter(part) for part in both_wgrads]
    down_wgrads = [blk_scatter(part) for part in down_wgrads]
    spans = ((1024, 1536), (1536, 2048), (0, 1024))
    for hidden, down in zip(hiddens[:-1], downs[:-1], strict=True):
        part = product_of(after(hidden, *second), down, transposed, mlp_part)
        mlp_part = {first: part(first, last) for first, last in spans}
    mlp_product = product_of(after(hiddens[-1], *third), downs[-1], transposed, mlp_part)
    mlp_product = {first: mlp_product(first, last) for first, last in spans}
    dres = layer_gather(
        *[after(t.astype(BF), down_last) for t in dresidual],
        [both_last] + [part[0] for part in mlp_product.values()],
    )
    mlp_state = scatter_start(lambda first, *_: mlp_product[first], (dres[1], dres[3]))
    dmix, dres_all = pieces_dot(dres, out_mat, transposed, BF)
    out_wgrad = wgrad(mix, dres_all).reshape(2, 2, share, width)
    out_away = pick(out_wgrad, 1 - y, 1)
    dmix = after(dmix, out_away, *mlp_state[2], *both_wgrads[:-1], *down_wgrads[:-1])
    draw, dgains = attend(scalars, raw, cos_table, sine_table, head_gains, groups, docs, dmix)
    mlp_out, mlp_third = scatter_end(mlp_state, (draw,))
    draw = after(draw, *mlp_third)
    beside = {}

    def after_attention(sent):
        beside["qkv"] = scaled_wgrad(units1_all, after(draw, *sent), gain_attn)
        return beside["qkv"], *both_wgrads, *down_wgrads

    state = scatter_start(product_of(draw, qkv_mat, transposed), (), after_attention)
    second = state[2]
    dnormed1, third = scatter_end(state)
    dnormed1 = [total_of(parts) for parts in dnormed1]
    out_wgrad = join(pick(out_wgrad, y, 1), after(over_y(out_away), draw), y, 0).reshape(4 * share, width)
    attn_wgrad = jnp.concatenate(
        [beside["qkv"].reshape(4, 8 * share, -1), out_wgrad.reshape(4, 4 * share, -1)], axis=1
    )
    attn_wgrad = after(attn_wgrad.reshape(48 * share, -1), *both_wgrads, *down_wgrads)
    attn_wgrad = blk_scatter(attn_wgrad)
    qkv_wgrad, out_low = attn_wgrad[: 8 * share], attn_wgrad[8 * share :].reshape(share, width)
    out_wgrad = sort_model(out_low, F32)

    gain_attn_grad = sum(jnp.sum(g * u, axis=0) for g, u in zip(dnormed1, unit_attn, strict=True))
    input_grad = [
        (t + norm_back(g, u, i, gain_attn)).astype(BF)
        for t, g, u, i in zip(dresidual, dnormed1, unit_attn, inverse_attn, strict=True)
    ]
    layer_out = [
        after((t + total_of(parts)).astype(BF), *second)
        for t, parts in zip(residual, mlp_out, strict=True)
    ]
    layer_out = rows_out(*layer_out, odd)
    layer_out = keep_rows(after(layer_out[0], *input_grad), layer_out[1], odd, BF)
    sent = by_bit(odd, *input_grad), by_bit(odd, *input_grad[::-1])
    input_got = rows_back(sent)

    own = after(jnp.concatenate([*both_wgrads, *down_wgrads], axis=1), *second)
    own = own.reshape(2, 2, width // 16, -1)
    own = after(trade(own, c_bit, over_c, 1), attn_wgrad, *third)
    own_got = over_x(pick(own, 1 - x_bit, 0))
    swapped = join(pick(own, x_bit, 0), own_got, x_bit, 0).reshape(4, width // 16, -1)
    input_grad = keep_rows(*input_got, odd, F32)
    gate_parts, upward_parts, down_parts = [], [], []
    for q in range(4):
        for tile in range(quarter // UNIT_TILE):
            cut = lambda i: swapped[q][:, i * UNIT_TILE : (i + 1) * UNIT_TILE]
            gate_parts.append(cut(2 * tile))
            upward_parts.append(cut(2 * tile + 1))
            down_parts.append(cut(2 * (quarter // UNIT_TILE) + tile))
    gate_wgrad, upward_wgrad, down_wgrad = (
        jnp.concatenate(parts, axis=1).astype(F32) for parts in (gate_parts, upward_parts, down_parts)
    )
    qkv_wgrad = qkv_wgrad.reshape(2, 2, 2, share, -1)
    qkv_wgrad = trade(trade(trade(qkv_wgrad, c_bit, over_c, 1), y, over_y, 2), x_bit, over_x, 0)
    qkv_wgrad = qkv_wgrad.reshape(8, share, -1)
    q_cols = groups * head
    query_wgrad = jnp.concatenate([qkv_wgrad[i][:, :q_cols] for i in range(8)], axis=1).astype(F32)
    key_wgrad = jnp.concatenate([qkv_wgrad[i][:, q_cols : q_cols + head] for i in range(8)], axis=1).astype(F32)
    value_wgrad = jnp.concatenate([qkv_wgrad[i][:, q_cols + head :] for i in range(8)], axis=1).astype(F32)

    dgains = jnp.sum(dgains, axis=0)
    small_grads = jnp.concatenate(
        [
            model_order(gain_attn_grad).reshape(32, -1),
            model_order(gain_mlp_grad).reshape(32, -1),
            dgains[0].reshape(32, -1),
            dgains[1].reshape(32, -1),
        ],
        axis=1,
    )
    small_grads = small_scatter(small_grads, coords, z, (own_got,))
    return (
        layer_out,
        input_grad,
        small_grads[:n_attn],
        small_grads[2 * n_attn : 2 * n_attn + n_head],
        small_grads[2 * n_attn + n_head :],
        query_wgrad,
        key_wgrad,
        value_wgrad,
        out_wgrad,
        small_grads[n_attn : 2 * n_attn],
        gate_wgrad,
        upward_wgrad,
        down_wgrad,
    )


def normalize(values, gain):
    inverse = lax.rsqrt(jnp.mean(values * values, axis=-1, keepdims=True) + EPSILON)
    return values * inverse * gain


def rotate(values, cos_table, sine_table):
    halfway = values.shape[-1] // 2
    turned = jnp.concatenate([-values[..., halfway:], values[..., :halfway]], axis=-1)
    return values * cos_table + turned * sine_table


def placement_of(lengths, offset, total):
    places = offset + jnp.arange(total, dtype=jnp.int32)
    ends = running_ends(lengths)
    before = (ends[:, None, :] <= places[None, :, None]).astype(jnp.int32)
    document = jnp.sum(before, axis=2)
    doc_start = jnp.sum(before * lengths[:, None, :], axis=2)
    return (document, places[None, :] - doc_start, places)


def rotary_tables(position, head_size):
    frequency = jnp.exp(
        jnp.arange(head_size // 2, dtype=jnp.float32) * (-2.0 / head_size) * math.log(ROPE_BASE)
    )
    angles = position.astype(jnp.float32)[..., None] * frequency
    angles = jnp.concatenate([angles, angles], axis=-1)
    return (jnp.cos(angles)[:, :, None, :], jnp.sin(angles)[:, :, None, :])


def head_path(raw_rows, gain, cos_table, sine_table):
    shaped = raw_rows.reshape(raw_rows.shape[0], raw_rows.shape[1], -1, gain.shape[0])
    return rotate(normalize(shaped, gain), cos_table, sine_table)


def block_size(total):
    return max((divisor for divisor in range(1, min(total, 512) + 1) if total % divisor == 0))


def silu_slope(gate_proj):
    logistic = jax.nn.sigmoid(gate_proj)
    return logistic * (1.0 + gate_proj * (1.0 - logistic))


def shards(
    hidden_in,
    out_grad,
    doc_lengths,
    norm_attn,
    query_gain,
    key_gain,
    query_weight,
    key_weight,
    value_weight,
    output_weight,
    norm_mlp,
    gate_weight,
    upward_weight,
    down_weight,
):
    attn_set = (
        lax.all_gather(query_weight, ("dp", "blk", "fsdp"), axis=0, tiled=True),
        lax.all_gather(key_weight, ("dp", "blk", "fsdp"), axis=0, tiled=True),
        lax.all_gather(value_weight, ("dp", "blk", "fsdp"), axis=0, tiled=True),
        lax.all_gather(output_weight, ("dp", "blk", "fsdp"), axis=0, tiled=True),
        lax.all_gather(norm_attn, ("dp", "blk", "fsdp"), axis=0, tiled=True),
        lax.all_gather(query_gain, ("dp", "blk", "fsdp"), axis=0, tiled=True),
        lax.all_gather(key_gain, ("dp", "blk", "fsdp"), axis=0, tiled=True),
        lax.all_gather(norm_mlp, ("dp", "blk", "fsdp"), axis=0, tiled=True),
    )
    query_mat, key_mat, value_mat, out_mat = (attn_set[0], attn_set[1], attn_set[2], attn_set[3])
    gain_attn = attn_set[4].astype(jnp.float32)
    gain_query = attn_set[5].astype(jnp.float32)
    gain_key = attn_set[6].astype(jnp.float32)
    gain_mlp = attn_set[7].astype(jnp.float32)
    gate_mat, upward_mat, down_mat = (
        lax.all_gather(gate_weight, ("dp", "blk"), axis=0, tiled=True),
        lax.all_gather(upward_weight, ("dp", "blk"), axis=0, tiled=True),
        lax.all_gather(down_weight, ("dp", "blk"), axis=0, tiled=True),
    )
    seq_count, local_rows, _width = hidden_in.shape
    head_size = gain_key.shape[0]
    heads_kv = key_mat.shape[1] // head_size
    heads_q = query_mat.shape[1] // head_size
    group_size = heads_q // heads_kv
    softmax_scale = 1.0 / math.sqrt(head_size)
    offset = lax.axis_index(("blk", "fsdp")) * local_rows
    query_doc, query_pos, query_place = placement_of(doc_lengths, offset, local_rows)
    cos_table, sine_table = rotary_tables(query_pos, head_size)
    layer_in = hidden_in.astype(jnp.float32)
    first_norm = normalize(layer_in, gain_attn).astype(jnp.bfloat16)
    query_raw = jnp.dot(first_norm, query_mat, preferred_element_type=jnp.float32)
    key_raw = jnp.dot(first_norm, key_mat, preferred_element_type=jnp.float32)
    value_rows = jnp.dot(first_norm, value_mat, preferred_element_type=jnp.float32).astype(
        jnp.bfloat16
    )
    query_rows = head_path(query_raw, gain_query, cos_table, sine_table).astype(jnp.bfloat16)
    query_rows = query_rows.reshape(seq_count, local_rows, heads_kv, group_size, head_size)
    key_rows = head_path(key_raw, gain_key, cos_table, sine_table).astype(jnp.bfloat16)
    key_rows = key_rows.reshape(seq_count, local_rows, heads_kv * head_size)

    def score_block(key_part, first_key):
        key_count = key_part.shape[1]
        key_heads = key_part.reshape(seq_count, key_count, heads_kv, head_size)
        scores = (
            jnp.einsum(
                "sckgd,spkd->skgcp", query_rows, key_heads, preferred_element_type=jnp.float32
            )
            * softmax_scale
        )
        key_doc, _key_pos, key_place = placement_of(doc_lengths, first_key, key_count)
        visible = (query_doc[:, None, None, :, None] == key_doc[:, None, None, None, :]) & (
            key_place[None, None, None, None, :] <= query_place[None, None, None, :, None]
        )
        return (scores, visible)

    def attend_block(running, key_part, value_part, first_key):
        run_max, run_total, run_sum = running
        scores, visible = score_block(key_part, first_key)
        masked = jnp.where(visible, scores, MASKED)
        new_max = jnp.maximum(run_max, jnp.max(masked, axis=-1))
        weights = jnp.where(visible, jnp.exp(masked - new_max[..., None]), 0.0)
        rescale = jnp.exp(run_max - new_max)
        value_heads = value_part.reshape(seq_count, -1, heads_kv, head_size)
        update = jnp.einsum(
            "skgcp,spkd->sckgd",
            weights.astype(jnp.bfloat16),
            value_heads,
            preferred_element_type=jnp.float32,
        )
        rescale_rows = jnp.transpose(rescale, (0, 3, 1, 2))[..., None]
        return (
            new_max,
            run_total * rescale + jnp.sum(weights, axis=-1),
            run_sum * rescale_rows + update,
        )

    start_carry = (
        jnp.full((seq_count, heads_kv, group_size, local_rows), MASKED, jnp.float32),
        jnp.zeros((seq_count, heads_kv, group_size, local_rows), jnp.float32),
        jnp.zeros((seq_count, local_rows, heads_kv, group_size, head_size), jnp.float32),
    )
    first_key = jnp.int32(0)
    key_part = lax.all_gather(key_rows, ("blk", "fsdp"), axis=1, tiled=True)
    value_part = lax.all_gather(value_rows, ("blk", "fsdp"), axis=1, tiled=True)
    piece_rows = key_part.shape[1]
    fold_block_len = block_size(piece_rows)

    def one_block(block_index, inner):
        begin_row = block_index * fold_block_len
        return attend_block(
            inner,
            lax.dynamic_slice_in_dim(key_part, begin_row, fold_block_len, 1),
            lax.dynamic_slice_in_dim(value_part, begin_row, fold_block_len, 1),
            first_key + begin_row,
        )

    running = lax.fori_loop(0, piece_rows // fold_block_len, one_block, start_carry)
    run_max, run_total, run_sum = running
    attn_mix = run_sum / jnp.transpose(run_total, (0, 3, 1, 2))[..., None]
    log_total = run_max + jnp.log(run_total)
    mix_rows = attn_mix.reshape(seq_count, local_rows, heads_q * head_size).astype(jnp.bfloat16)
    residual = layer_in + jnp.dot(mix_rows, out_mat, preferred_element_type=jnp.float32)
    second_norm = normalize(residual, gain_mlp).astype(jnp.bfloat16)
    pair_rows = lax.all_gather(second_norm, "fsdp", axis=1, tiled=True)
    gate_proj = jnp.dot(pair_rows, gate_mat, preferred_element_type=jnp.float32)
    upward_proj = jnp.dot(pair_rows, upward_mat, preferred_element_type=jnp.float32)
    hidden_rows = (jax.nn.silu(gate_proj) * upward_proj).astype(jnp.bfloat16)
    down_part = jnp.einsum("scf,df->scd", hidden_rows, down_mat, preferred_element_type=jnp.float32)
    mlp_out = lax.psum_scatter(
        down_part.astype(jnp.bfloat16), "fsdp", scatter_dimension=1, tiled=True
    ).astype(jnp.float32)
    layer_out = (residual + mlp_out).astype(jnp.bfloat16)
    top_grad = out_grad.astype(jnp.float32)
    gate_back, upward_back, down_back = (
        lax.all_gather(gate_weight, ("dp", "blk"), axis=0, tiled=True),
        lax.all_gather(upward_weight, ("dp", "blk"), axis=0, tiled=True),
        lax.all_gather(down_weight, ("dp", "blk"), axis=0, tiled=True),
    )
    pair_grad = lax.all_gather(out_grad, "fsdp", axis=1, tiled=True)
    hidden_grad = jnp.einsum(
        "scd,df->scf", pair_grad, down_back, preferred_element_type=jnp.float32
    )
    down_wgrad = jnp.einsum(
        "scd,scf->df", pair_grad, hidden_rows, preferred_element_type=jnp.float32
    )
    gate_grad = (hidden_grad * upward_proj * silu_slope(gate_proj)).astype(jnp.bfloat16)
    upward_grad = (hidden_grad * jax.nn.silu(gate_proj)).astype(jnp.bfloat16)
    gate_wgrad = jnp.einsum("scd,scf->df", pair_rows, gate_grad, preferred_element_type=jnp.float32)
    upward_wgrad = jnp.einsum(
        "scd,scf->df", pair_rows, upward_grad, preferred_element_type=jnp.float32
    )
    norm_part = jnp.einsum("scf,df->scd", gate_grad, gate_back, preferred_element_type=jnp.float32)
    norm_part = norm_part + jnp.einsum(
        "scf,df->scd", upward_grad, upward_back, preferred_element_type=jnp.float32
    )
    second_grad = lax.psum_scatter(
        norm_part.astype(jnp.bfloat16), "fsdp", scatter_dimension=1, tiled=True
    ).astype(jnp.float32)
    mlp_wgrads = (
        lax.psum_scatter(gate_wgrad, ("dp", "blk"), scatter_dimension=0, tiled=True),
        lax.psum_scatter(upward_wgrad, ("dp", "blk"), scatter_dimension=0, tiled=True),
        lax.psum_scatter(down_wgrad, ("dp", "blk"), scatter_dimension=0, tiled=True),
    )
    _second_value, second_pull = jax.vjp(normalize, residual, gain_mlp)
    residual_part, gain_mlp_grad = second_pull(second_grad)
    residual_grad = top_grad + residual_part
    query_back, key_back, value_back, out_back = (
        lax.all_gather(query_weight, ("dp", "blk", "fsdp"), axis=0, tiled=True),
        lax.all_gather(key_weight, ("dp", "blk", "fsdp"), axis=0, tiled=True),
        lax.all_gather(value_weight, ("dp", "blk", "fsdp"), axis=0, tiled=True),
        lax.all_gather(output_weight, ("dp", "blk", "fsdp"), axis=0, tiled=True),
    )
    residual_low = residual_grad.astype(jnp.bfloat16)
    out_wgrad = jnp.einsum(
        "sce,scd->ed", mix_rows, residual_low, preferred_element_type=jnp.float32
    )
    mix_grad = jnp.einsum("scd,ed->sce", residual_low, out_back, preferred_element_type=jnp.float32)
    mix_grad = mix_grad.astype(jnp.bfloat16).reshape(
        seq_count, local_rows, heads_kv, group_size, head_size
    )
    delta = jnp.transpose(jnp.sum(mix_grad.astype(jnp.float32) * attn_mix, axis=-1), (0, 2, 3, 1))
    key_all, value_all = (
        lax.all_gather(key_rows, ("blk", "fsdp"), axis=1, tiled=True),
        lax.all_gather(value_rows, ("blk", "fsdp"), axis=1, tiled=True),
    )
    full_rows = key_all.shape[1]
    block_len = block_size(full_rows)

    def back_block(block_index, running_back):
        query_acc, key_buffer, value_buffer = running_back
        first_key = block_index * block_len
        key_part = lax.dynamic_slice_in_dim(key_all, first_key, block_len, 1)
        value_part = lax.dynamic_slice_in_dim(value_all, first_key, block_len, 1)
        key_heads = key_part.reshape(seq_count, block_len, heads_kv, head_size)
        value_heads = value_part.reshape(seq_count, block_len, heads_kv, head_size)
        scores, visible = score_block(key_part, first_key)
        probs = jnp.where(
            visible, jnp.exp(jnp.where(visible, scores, MASKED) - log_total[..., None]), 0.0
        )
        probs_grad = jnp.einsum(
            "sckgd,spkd->skgcp", mix_grad, value_heads, preferred_element_type=jnp.float32
        )
        score_grad = (probs * (probs_grad - delta[..., None])).astype(jnp.bfloat16)
        query_acc = (
            query_acc
            + jnp.einsum(
                "skgcp,spkd->sckgd", score_grad, key_heads, preferred_element_type=jnp.float32
            )
            * softmax_scale
        )
        key_piece = (
            jnp.einsum(
                "skgcp,sckgd->spkd", score_grad, query_rows, preferred_element_type=jnp.float32
            )
            * softmax_scale
        )
        value_piece = jnp.einsum(
            "skgcp,sckgd->spkd",
            probs.astype(jnp.bfloat16),
            mix_grad,
            preferred_element_type=jnp.float32,
        )
        key_buffer = lax.dynamic_update_slice_in_dim(
            key_buffer, key_piece.reshape(seq_count, block_len, -1), first_key, 1
        )
        value_buffer = lax.dynamic_update_slice_in_dim(
            value_buffer, value_piece.reshape(seq_count, block_len, -1), first_key, 1
        )
        return (query_acc, key_buffer, value_buffer)

    back_init = (
        jnp.zeros((seq_count, local_rows, heads_kv, group_size, head_size), jnp.float32),
        jnp.zeros((seq_count, full_rows, heads_kv * head_size), jnp.float32),
        jnp.zeros((seq_count, full_rows, heads_kv * head_size), jnp.float32),
    )
    query_acc, key_buffer, value_buffer = lax.fori_loop(
        0, full_rows // block_len, back_block, back_init
    )
    key_grad, value_grad = (
        lax.psum_scatter(
            key_buffer.astype(jnp.bfloat16), ("blk", "fsdp"), scatter_dimension=1, tiled=True
        ).astype(jnp.float32),
        lax.psum_scatter(
            value_buffer.astype(jnp.bfloat16), ("blk", "fsdp"), scatter_dimension=1, tiled=True
        ).astype(jnp.float32),
    )

    def query_path(raw_rows, gain):
        return head_path(raw_rows, gain, cos_table, sine_table)

    _query_value, query_pull = jax.vjp(query_path, query_raw, gain_query)
    query_raw_grad, gain_query_grad = query_pull(
        query_acc.reshape(seq_count, local_rows, heads_q, head_size)
    )
    _key_value, key_pull = jax.vjp(query_path, key_raw, gain_key)
    key_raw_grad, gain_key_grad = key_pull(
        key_grad.reshape(seq_count, local_rows, heads_kv, head_size)
    )
    query_low = query_raw_grad.astype(jnp.bfloat16)
    key_low = key_raw_grad.astype(jnp.bfloat16)
    value_low = value_grad.astype(jnp.bfloat16)
    query_wgrad = jnp.einsum(
        "scd,sce->de", first_norm, query_low, preferred_element_type=jnp.float32
    )
    key_wgrad = jnp.einsum("scd,sce->de", first_norm, key_low, preferred_element_type=jnp.float32)
    value_wgrad = jnp.einsum(
        "scd,sce->de", first_norm, value_low, preferred_element_type=jnp.float32
    )
    first_grad = jnp.einsum(
        "sce,de->scd", query_low, query_back, preferred_element_type=jnp.float32
    )
    first_grad = first_grad + jnp.einsum(
        "sce,de->scd", key_low, key_back, preferred_element_type=jnp.float32
    )
    first_grad = first_grad + jnp.einsum(
        "sce,de->scd", value_low, value_back, preferred_element_type=jnp.float32
    )
    _first_value, first_pull = jax.vjp(normalize, layer_in, gain_attn)
    layer_part, gain_attn_grad = first_pull(first_grad)
    input_grad = residual_grad + layer_part
    attn_wgrads = (
        lax.psum_scatter(query_wgrad, ("dp", "blk", "fsdp"), scatter_dimension=0, tiled=True),
        lax.psum_scatter(key_wgrad, ("dp", "blk", "fsdp"), scatter_dimension=0, tiled=True),
        lax.psum_scatter(value_wgrad, ("dp", "blk", "fsdp"), scatter_dimension=0, tiled=True),
        lax.psum_scatter(out_wgrad, ("dp", "blk", "fsdp"), scatter_dimension=0, tiled=True),
        lax.psum_scatter(gain_attn_grad, ("dp", "blk", "fsdp"), scatter_dimension=0, tiled=True),
        lax.psum_scatter(gain_query_grad, ("dp", "blk", "fsdp"), scatter_dimension=0, tiled=True),
        lax.psum_scatter(gain_key_grad, ("dp", "blk", "fsdp"), scatter_dimension=0, tiled=True),
        lax.psum_scatter(gain_mlp_grad, ("dp", "blk", "fsdp"), scatter_dimension=0, tiled=True),
    )
    return (
        layer_out,
        input_grad,
        attn_wgrads[4],
        attn_wgrads[5],
        attn_wgrads[6],
        attn_wgrads[0],
        attn_wgrads[1],
        attn_wgrads[2],
        attn_wgrads[3],
        attn_wgrads[7],
        mlp_wgrads[0],
        mlp_wgrads[1],
        mlp_wgrads[2],
    )


def solution(mesh):
    sizes = dict(mesh.shape)
    layered = (sizes["dp"], sizes["blk"], sizes["fsdp"]) == (4, 4, 2)
    return jax.shard_map(
        layer_shards if layered else shards,
        mesh=mesh,
        in_specs=(
            P("dp", ("blk", "fsdp"), None),
            P("dp", ("blk", "fsdp"), None),
            P("dp", None),
            P(("dp", "blk", "fsdp")),
            P(("dp", "blk", "fsdp")),
            P(("dp", "blk", "fsdp")),
            P(("dp", "blk", "fsdp"), None),
            P(("dp", "blk", "fsdp"), None),
            P(("dp", "blk", "fsdp"), None),
            P(("dp", "blk", "fsdp"), None),
            P(("dp", "blk", "fsdp")),
            P(("dp", "blk"), "fsdp"),
            P(("dp", "blk"), "fsdp"),
            P(("dp", "blk"), "fsdp"),
        ),
        out_specs=(
            P("dp", ("blk", "fsdp"), None),
            P("dp", ("blk", "fsdp"), None),
            P(("dp", "blk", "fsdp")),
            P(("dp", "blk", "fsdp")),
            P(("dp", "blk", "fsdp")),
            P(("dp", "blk", "fsdp"), None),
            P(("dp", "blk", "fsdp"), None),
            P(("dp", "blk", "fsdp"), None),
            P(("dp", "blk", "fsdp"), None),
            P(("dp", "blk", "fsdp")),
            P(("dp", "blk"), "fsdp"),
            P(("dp", "blk"), "fsdp"),
            P(("dp", "blk"), "fsdp"),
        ),
        check_vma=False,
    )
```

```python
import functools
import math

import jax
import jax.numpy as jnp
from jax import lax
from jax.experimental import pallas as pl
from jax.experimental.pallas import tpu as pltpu
from jax.sharding import PartitionSpec as P

EPSILON = 1e-06
ROPE_BASE = 1000000.0
MASKED = -1e30
BF = jnp.bfloat16
F32 = jnp.float32
EVERY = ("dp", "blk", "fsdp")


def running_ends(lengths):
    parts = [lengths[..., :1]]
    for index in range(1, lengths.shape[-1]):
        parts.append(parts[-1] + lengths[..., index : index + 1])
    return jnp.concatenate(parts, axis=-1)


SWAP_X = [(0, 2), (2, 0), (1, 3), (3, 1)]
SWAP_C = [(0, 1), (1, 0), (2, 3), (3, 2)]
SWAP_Y = [(0, 1), (1, 0)]
BLOCK = 128
PIECES = 8


def over_x(value):
    return lax.ppermute(value, "dp", SWAP_X)


def over_c(value):
    return lax.ppermute(value, "dp", SWAP_C)


def over_y(value):
    return lax.ppermute(value, "fsdp", SWAP_Y)


def after(value, *before):
    return lax.optimization_barrier((value, *before))[0]


def sum_low(*parts):
    return functools.reduce(lambda a, b: a + b, [p.astype(F32) for p in parts]).astype(BF)


def by_bit(bit, zero, one):
    return jnp.where(bit == 1, one, zero)


def pick(value, index, axis):
    return lax.dynamic_index_in_dim(value, index, axis, keepdims=False)


def flip_where(bit, value, axis):
    first, second = jnp.split(value, 2, axis)
    return jnp.where(bit == 1, jnp.concatenate([second, first], axis), value)


def together(*values):
    return lax.optimization_barrier(values)


def layer_gather(low, high, core_after=()):
    low_x, high_y = together(over_x(low), over_y(high))
    low_row, high_row = together(jnp.concatenate([low, low_x]), jnp.concatenate([high, high_y]))
    low_both, high_both = together(over_y(low_row), over_x(high_row))
    near = [low_row, low_both, high_row, high_both]
    last = [after(piece, *core_after) if core_after else piece for piece in (low_both, high_both)]
    sent = [low_row, last[0], high_row, last[1]]
    return near + [over_c(piece) for piece in sent]


def scatter_start(product, core_after=(), middle=None):
    sent_low, sent_high = product(1024, 1536), product(1536, 2048)
    more = middle((sent_low[0], sent_high[0])) if middle else ()
    here = product(0, 1024, sent_low[0], sent_high[0], *more)
    far_low, far_high = together(
        over_c(after(sent_low[0], *core_after)), over_c(after(sent_high[0], *core_after))
    )
    second = together(
        sum_low(*[part[256:512] for part in here], far_low[256:]),
        sum_low(*[part[768:] for part in here], far_high[256:]),
    )
    low_back, high_back = together(over_y(second[0]), over_x(second[1]))
    return here, (far_low, far_high), second, (low_back, high_back)


def scatter_end(state, before=()):
    here, (far_low, far_high), _, (low_back, high_back) = state
    if before:
        low_back, high_back, *_ = together(low_back, high_back, *before)
    third = together(
        sum_low(*[part[128:256] for part in here], far_low[128:256], low_back[128:]),
        sum_low(*[part[640:768] for part in here], far_high[128:256], high_back[128:]),
    )
    low_last, high_last = together(over_x(third[0]), over_y(third[1]))
    parts = (
        (*[part[:128] for part in here], far_low[:128], low_back[:128], low_last),
        (*[part[512:640] for part in here], far_high[:128], high_back[:128], high_last),
    )
    return parts, third


def product_of(rows, matrix, dims, more=None):
    def product(first, last, *before):
        part = rows[first:last]
        part = after(part, *before) if before else part
        out = lax.dot_general(part, matrix, dims, preferred_element_type=F32)
        if more is None or first == 0:
            return [out.astype(BF)] + (more[first] if more else [])
        return [(out + more[first][0].astype(F32)).astype(BF)]

    return product


def total_of(parts):
    return functools.reduce(lambda a, b: a + b, [p.astype(F32) for p in parts])


def blk_gather(own):
    return lax.all_gather(own, "blk", axis=0, tiled=True)


def blk_scatter(partial):
    return lax.psum_scatter(partial, "blk", scatter_dimension=0, tiled=True)


def swap_z(value, step):
    return lax.ppermute(value, "blk", [(z, z ^ step) for z in range(4)])


def small_gather(value, coords, z):
    x_bit, c_bit, y_bit = coords
    for bit, move in (
        (y_bit, over_y),
        (c_bit, over_c),
        (x_bit, over_x),
        (z % 2, functools.partial(swap_z, step=1)),
        (z // 2, functools.partial(swap_z, step=2)),
    ):
        got = move(value)
        value = flip_where(bit, jnp.stack([value, got]), 0)
    return value.reshape(4, 2, 2, 2, -1), got


def small_scatter(value, coords, z, before):
    x_bit, c_bit, y_bit = coords
    value = value.reshape(2, 2, 2, 2, 2, -1)
    for bit, move, axis in ((x_bit, over_x, 0), (c_bit, over_c, 0), (y_bit, over_y, 2)):
        value = pick(value, bit, axis) + move(pick(value, 1 - bit, axis))
    value = after(value, *before)
    for bit, step in ((z // 2, 2), (z % 2, 1)):
        value = pick(value, bit, 0) + swap_z(pick(value, 1 - bit, 0), step)
    return value


def width_blocks(value):
    step = value.shape[-1] // 16
    return [value[..., i * step : (i + 1) * step] for i in range(16)]


def model_order(value):
    blocks = width_blocks(value)
    return jnp.concatenate([blocks[j * 4 + i] for i in range(4) for j in range(4)], axis=-1)


def trade(value, bit, move, axis):
    keep, got = pick(value, bit, axis), move(pick(value, 1 - bit, axis))
    return by_bit(bit, jnp.stack([keep, got], axis), jnp.stack([got, keep], axis))


def join(keep, got, bit, axis):
    return by_bit(bit, jnp.stack([keep, got], axis), jnp.stack([got, keep], axis))


def row_moves():
    first, second = [], []
    for d in range(4):
        for z in range(4):
            for y in range(2):
                source = d * 8 + z * 2 + y
                target = (d // 2) * 2 + z // 2
                first.append((source, target * 8 + (2 * (d % 2) + z % 2) * 2 + y))
                second.append((source, target * 8 + (2 * (d % 2) + 1 - z % 2) * 2 + y))
    return first, second


def sort_width(read, write, width):
    step = width // 16
    for i in range(4):
        for j in range(4):
            write(slice((i * 4 + j) * step, (i * 4 + j + 1) * step), read(slice((j * 4 + i) * step, (j * 4 + i + 1) * step)))


def send_rows_kernel(odd_ref, value_ref, first_ref, second_ref):
    odd = odd_ref[0]
    for out, at in ((first_ref, odd), (second_ref, 1 - odd)):

        def write(cols, value, out=out):
            out[:, cols] = value

        sort_width(lambda cols, at=at: value_ref[at, :, cols], write, out.shape[1])


def send_rows(value, odd):
    shape = jax.ShapeDtypeStruct(value.shape[1:], value.dtype)
    return pl.pallas_call(
        send_rows_kernel,
        in_specs=[pl.BlockSpec(memory_space=pltpu.SMEM), pl.BlockSpec(memory_space=pltpu.VMEM)],
        out_specs=[pl.BlockSpec(memory_space=pltpu.VMEM)] * 2,
        out_shape=[shape, shape],
    )(odd.reshape(1), value)


def keep_rows_kernel(odd_ref, first_ref, second_ref, out_ref):
    odd = odd_ref[0]
    for got, at in ((first_ref, odd), (second_ref, 1 - odd)):

        def write(cols, value, at=at):
            out_ref[at, :, cols] = value.astype(out_ref.dtype)

        sort_width(lambda cols, got=got: got[:, cols], write, got.shape[1])


def keep_rows(first, second, odd, dtype):
    return pl.pallas_call(
        keep_rows_kernel,
        in_specs=[pl.BlockSpec(memory_space=pltpu.SMEM)] + [pl.BlockSpec(memory_space=pltpu.VMEM)] * 2,
        out_specs=pl.BlockSpec(memory_space=pltpu.VMEM),
        out_shape=jax.ShapeDtypeStruct((2, *first.shape), dtype),
    )(odd.reshape(1), first, second)


def sort_kernel(value_ref, out_ref):
    def write(cols, value):
        out_ref[:, cols] = value.astype(out_ref.dtype)

    sort_width(lambda cols: value_ref[:, cols], write, value_ref.shape[1])


def sort_model(value, dtype):
    return pl.pallas_call(
        sort_kernel,
        in_specs=[pl.BlockSpec(memory_space=pltpu.VMEM)],
        out_specs=pl.BlockSpec(memory_space=pltpu.VMEM),
        out_shape=jax.ShapeDtypeStruct(value.shape, dtype),
    )(value)


def rows_in(sent, odd):
    moves = row_moves()
    got_first = lax.ppermute(sent[0], EVERY, moves[0])
    got_second = lax.ppermute(sent[1], EVERY, moves[1])
    return by_bit(odd, got_first, got_second), by_bit(odd, got_second, got_first)


def rows_back(sent):
    moves = row_moves()
    return [lax.ppermute(s, EVERY, [(b, a) for a, b in m]) for s, m in zip(sent, moves, strict=True)]


def rows_out(low, high, odd):
    return rows_back((by_bit(odd, low, high), by_bit(odd, high, low)))


def block_rows(scalars, row, block):
    c_bit, y_bit = scalars[0], scalars[1]
    far_c = jnp.where(c_bit == (block >> 2), 0, 1)
    far_y = jnp.where(y_bit == (block & 1), 0, 1)
    if (block >> 1) & 1:
        at = far_c * 8 + 4 + row * 2 + far_y
    else:
        at = far_c * 8 + far_y * 2 + row
    return pl.ds(pl.multiple_of(at * BLOCK, BLOCK), BLOCK)


def swap_halves(value):
    return pltpu.roll(value, value.shape[-1] // 2, 1)


def head_forward(raw, gain, cos, sine):
    inverse = lax.rsqrt(jnp.mean(raw * raw, axis=-1, keepdims=True) + EPSILON)
    scaled = raw * inverse * gain
    return scaled * cos + swap_halves(scaled) * sine


def head_backward(grad, raw, gain, cos, sine):
    inverse = lax.rsqrt(jnp.mean(raw * raw, axis=-1, keepdims=True) + EPSILON)
    unit = raw * inverse
    back = grad * cos + swap_halves(grad * sine)
    gain_grad = jnp.sum(back * unit, axis=0, keepdims=True)
    scaled = back * gain
    return inverse * (scaled - unit * jnp.mean(scaled * unit, axis=-1, keepdims=True)), gain_grad


def visible_pairs(scalars, row, first_query, queries, keys, docs):
    place = first_query + lax.broadcasted_iota(jnp.int32, (queries, 1), 0)
    start = jnp.zeros_like(place)
    for doc in range(docs - 1):
        end = scalars[2 + row * docs + doc]
        start = jnp.where(place >= end, end, start)
    key_place = lax.broadcasted_iota(jnp.int32, (queries, keys), 1)
    return (key_place >= start) & (key_place <= place)


def fetch(pieces, held, sems, base=0):
    size = held.shape[0] // len(pieces)
    return [
        pltpu.make_async_copy(piece, held.at[pl.ds(i * size, size), :], sems.at[base + i])
        for i, piece in enumerate(pieces)
    ]


def load_row(scalars, row, raw_ref, cos_ref, sine_ref, gain_ref, q_s, k_s, v_s, groups, blocks):
    width = 128
    for block in range(blocks):
        rel = block_rows(scalars, row, block)
        rows = slice(block * BLOCK, block * BLOCK + BLOCK)
        cos, sine = cos_ref[0, rows, :], sine_ref[0, rows, :]
        for g in range(groups):
            raw = raw_ref[rel, g * width : (g + 1) * width]
            q_s[rows, g * width : (g + 1) * width] = head_forward(
                raw, gain_ref[0:1, :], cos, sine
            ).astype(BF)
        raw = raw_ref[rel, groups * width : (groups + 1) * width]
        k_s[rows, :] = head_forward(raw, gain_ref[1:2, :], cos, sine).astype(BF)
        v_s[rows, :] = raw_ref[rel, (groups + 1) * width : (groups + 2) * width].astype(BF)


ROWS_C = (((1,), (1,)), ((), ()))
COLS_C = (((0,), (0,)), ((), ()))


def attend_kernel(scalars, cos_ref, sine_ref, gain_ref, *refs, groups, docs, step):
    raw_s, mix_ref, q_s, k_s, v_s = refs
    row = pl.program_id(0)
    total = k_s.shape[0]
    load_row(scalars, row, raw_s, cos_ref, sine_ref, gain_ref, q_s, k_s, v_s, groups, total // BLOCK)
    scale = 1.0 / math.sqrt(128)
    for first in range(0, total, step):
        keys = first + step
        visible = visible_pairs(scalars, row, first, step, keys, docs)
        for g in range(groups):
            query = q_s[first : first + step, g * 128 : (g + 1) * 128]
            scores = lax.dot_general(query, k_s[:keys, :], ROWS_C, preferred_element_type=F32) * scale
            scores = jnp.where(visible, scores, MASKED)
            weights = jnp.exp(scores - jnp.max(scores, axis=-1, keepdims=True))
            norm = jnp.sum(weights, axis=-1, keepdims=True)
            mixed = jnp.dot(weights.astype(BF), v_s[:keys, :], preferred_element_type=F32) / norm
            for part in range(step // BLOCK):
                rel = block_rows(scalars, row, first // BLOCK + part)
                mix_ref[rel, g * 128 : (g + 1) * 128] = mixed[part * BLOCK : (part + 1) * BLOCK].astype(BF)


def attend_back_kernel(scalars, cos_ref, sine_ref, gain_ref, *refs, groups, docs, step):
    raw_s, dmix_s, draw_ref, dgain_ref, q_s, k_s, v_s, dk_s, dv_s = refs
    row = pl.program_id(0)
    total = k_s.shape[0]
    load_row(scalars, row, raw_s, cos_ref, sine_ref, gain_ref, q_s, k_s, v_s, groups, total // BLOCK)
    scale = 1.0 / math.sqrt(128)
    dk_s[...] = jnp.zeros_like(dk_s)
    dv_s[...] = jnp.zeros_like(dv_s)
    query_gain = jnp.zeros((1, 128), F32)
    for first in range(0, total, step):
        keys = first + step
        visible = visible_pairs(scalars, row, first, step, keys, docs)
        order = [block_rows(scalars, row, first // BLOCK + part) for part in range(step // BLOCK)]
        for g in range(groups):
            cols = slice(g * 128, (g + 1) * 128)
            query = q_s[first : first + step, cols]
            dmix = jnp.concatenate([dmix_s[rel, cols] for rel in order], axis=0)
            scores = lax.dot_general(query, k_s[:keys, :], ROWS_C, preferred_element_type=F32) * scale
            scores = jnp.where(visible, scores, MASKED)
            weights = jnp.exp(scores - jnp.max(scores, axis=-1, keepdims=True))
            probs = weights / jnp.sum(weights, axis=-1, keepdims=True)
            dprobs = lax.dot_general(dmix, v_s[:keys, :], ROWS_C, preferred_element_type=F32)
            delta = jnp.sum(probs * dprobs, axis=-1, keepdims=True)
            dscores = (probs * (dprobs - delta)).astype(BF)
            dquery = jnp.dot(dscores, k_s[:keys, :], preferred_element_type=F32) * scale
            dk_s[:keys, :] += lax.dot_general(dscores, query, COLS_C, preferred_element_type=F32)
            dv_s[:keys, :] += lax.dot_general(probs.astype(BF), dmix, COLS_C, preferred_element_type=F32)
            for part, rel in enumerate(order):
                rows = slice(first + part * BLOCK, first + (part + 1) * BLOCK)
                draw, gain_part = head_backward(
                    dquery[part * BLOCK : (part + 1) * BLOCK], raw_s[rel, cols], gain_ref[0:1, :],
                    cos_ref[0, rows, :], sine_ref[0, rows, :],
                )
                draw_ref[rel, cols] = draw.astype(BF)
                query_gain += gain_part
    key_gain = jnp.zeros((1, 128), F32)
    cols = slice(groups * 128, (groups + 1) * 128)
    for block in range(total // BLOCK):
        rel = block_rows(scalars, row, block)
        rows = slice(block * BLOCK, (block + 1) * BLOCK)
        draw, gain_part = head_backward(
            dk_s[rows, :] * scale, raw_s[rel, cols], gain_ref[1:2, :], cos_ref[0, rows, :], sine_ref[0, rows, :]
        )
        draw_ref[rel, cols] = draw.astype(BF)
        draw_ref[rel, (groups + 1) * 128 : (groups + 2) * 128] = dv_s[rows, :].astype(BF)
        key_gain += gain_part
    dgain_ref[0, :, :] = jnp.concatenate([query_gain, key_gain, jnp.zeros((6, 128), F32)], axis=0)


ATTEND_STEP = 256


def attend(scalars, raw, cos, sine, gains, groups, docs, dmix=None):
    total, width = cos.shape[1], raw.shape[1]
    by_row = pl.BlockSpec((1, total, 128), lambda r, s: (r, 0, 0))
    back = dmix is not None
    given = [raw, dmix] if back else [raw]
    once = lambda columns: pl.BlockSpec((2 * total, columns), lambda r, s: (0, 0))
    out_specs = [once(width if back else groups * 128)]
    out_shape = [jax.ShapeDtypeStruct((2 * total, width if back else groups * 128), BF)]
    if back:
        out_specs.append(pl.BlockSpec((1, 8, 128), lambda r, s: (r, 0, 0)))
        out_shape.append(jax.ShapeDtypeStruct((2, 8, 128), F32))
    scratch = [
        pltpu.VMEM((total, groups * 128), BF),
        pltpu.VMEM((total, 128), BF),
        pltpu.VMEM((total, 128), BF),
    ]
    if back:
        scratch += [pltpu.VMEM((total, 128), F32), pltpu.VMEM((total, 128), F32)]
    return pl.pallas_call(
        functools.partial(
            attend_back_kernel if back else attend_kernel, groups=groups, docs=docs, step=ATTEND_STEP
        ),
        grid_spec=pltpu.PrefetchScalarGridSpec(
            num_scalar_prefetch=1,
            grid=(2,),
            in_specs=[by_row, by_row, pl.BlockSpec((8, 128), lambda r, s: (0, 0))]
            + [once(part.shape[1]) for part in given],
            out_specs=out_specs,
            scratch_shapes=scratch,
        ),
        out_shape=out_shape,
        compiler_params=pltpu.CompilerParams(vmem_limit_bytes=40 * 2**20),
        cost_estimate=pl.CostEstimate(
            flops=groups * total * total * 128 * 2 * (5 if back else 2) * 2 * 5 // 8,
            bytes_accessed=(40 if back else 12) * 2**20,
            transcendentals=groups * total * total * 2,
        ),
    )(scalars, cos, sine, gains, *given)


def pieces_kernel(matrix_ref, *refs, dims):
    pieces, (out_ref, whole_ref, held, sems, out_sem) = refs[:PIECES], refs[PIECES:]
    copies = fetch(pieces, held, sems)
    for copy in copies:
        copy.start()
    size = held.shape[0] // PIECES
    for at, copy in enumerate(copies):
        copy.wait()
        rows = slice(at * size, (at + 1) * size)
        out_ref[rows, :] = lax.dot_general(
            held[rows, :], matrix_ref[...], dims, preferred_element_type=F32
        ).astype(out_ref.dtype)
    out = pltpu.make_async_copy(held, whole_ref, out_sem)
    out.start()
    out.wait()


def pieces_dot(pieces, matrix, dims, dtype):
    rows, width = pieces[0].shape
    columns = matrix.shape[1 - dims[0][1][0]]
    vmem, anywhere = pl.BlockSpec(memory_space=pltpu.VMEM), pl.BlockSpec(memory_space=pl.ANY)
    return pl.pallas_call(
        functools.partial(pieces_kernel, dims=dims),
        in_specs=[vmem] + [anywhere] * PIECES,
        out_specs=[vmem, anywhere],
        out_shape=[
            jax.ShapeDtypeStruct((PIECES * rows, columns), dtype),
            jax.ShapeDtypeStruct((PIECES * rows, width), BF),
        ],
        scratch_shapes=[
            pltpu.VMEM((PIECES * rows, width), BF),
            pltpu.SemaphoreType.DMA((PIECES,)),
            pltpu.SemaphoreType.DMA,
        ],
        compiler_params=pltpu.CompilerParams(vmem_limit_bytes=32 * 2**20),
        cost_estimate=pl.CostEstimate(
            flops=2 * PIECES * rows * width * columns,
            bytes_accessed=4 * PIECES * rows * width + 4 * PIECES * rows * columns,
            transcendentals=0,
        ),
    )(matrix, *pieces)


UNIT_TILE = 256
TOKEN_TILE = 512


def units_kernel(both_ref, down_ref, *refs, given):
    normed, tops = refs[:given], refs[given : 2 * given]
    hidden_ref, dboth_ref = refs[2 * given : 2 * given + 2]
    *wholes, normed_s, top_s, sems, out_sems = refs[2 * given + 2 :]
    at = pl.program_id(0)
    last = pl.num_programs(0) - 1
    size = normed_s.shape[0] // PIECES
    if given == 1:
        normed, tops = ([r[0].at[pl.ds(i * size, size), :] for i in range(PIECES)] for r in (normed, tops))
    copies = fetch(normed, normed_s, sems), fetch(tops, top_s, sems, PIECES)
    outs = [
        pltpu.make_async_copy(held, whole, out_sems.at[i])
        for i, (held, whole) in enumerate(zip((normed_s, top_s), wholes))
    ]

    @pl.when(at == 0)
    def _():
        for one, other in zip(*copies, strict=True):
            one.start()
            other.start()

    per = TOKEN_TILE // size

    def work(tile):
        rows = slice(tile * TOKEN_TILE, (tile + 1) * TOKEN_TILE)
        both = jnp.dot(normed_s[rows, :], both_ref[...], preferred_element_type=F32)
        gate, upward = both[:, :UNIT_TILE], both[:, UNIT_TILE:]
        dhidden = jnp.dot(top_s[rows, :], down_ref[...], preferred_element_type=F32)
        logistic = 1.0 / (1.0 + jnp.exp(-gate))
        swish = gate * logistic
        hidden_ref[rows, :] = (swish * upward).astype(BF)
        dgate = dhidden * upward * (logistic * (1.0 + gate * (1.0 - logistic)))
        dboth_ref[rows, :UNIT_TILE] = dgate.astype(BF)
        dboth_ref[rows, UNIT_TILE:] = (dhidden * swish).astype(BF)

    @pl.when(at == 0)
    def _():
        for tile in range(normed_s.shape[0] // TOKEN_TILE):
            for piece in range(tile * per, (tile + 1) * per):
                copies[0][piece].wait()
                copies[1][piece].wait()
            work(tile)

    @pl.when(at > 0)
    def _():
        for tile in range(normed_s.shape[0] // TOKEN_TILE):
            work(tile)

    if outs:

        @pl.when(at == 0)
        def _():
            for out in outs:
                out.start()

        @pl.when(at == last)
        def _():
            for out in outs:
                out.wait()


def units_pass(normed, tops, mat):
    given = len(normed)
    width, units = mat.shape[0], mat.shape[1] // 3
    tiles = units // UNIT_TILE
    tokens = given * normed[0].shape[0]
    anywhere = pl.BlockSpec(memory_space=pl.ANY)
    whole = jax.ShapeDtypeStruct((tokens, width), BF)
    wholes = 0 if given == 1 else 2
    return pl.pallas_call(
        functools.partial(units_kernel, given=given),
        grid=(tiles,),
        in_specs=[
            pl.BlockSpec((width, 2 * UNIT_TILE), lambda i: (0, i)),
            pl.BlockSpec((width, UNIT_TILE), lambda i: (0, 2 * tiles + i)),
        ]
        + [anywhere] * (2 * given),
        out_specs=[
            pl.BlockSpec((tokens, UNIT_TILE), lambda i: (0, i)),
            pl.BlockSpec((tokens, 2 * UNIT_TILE), lambda i: (0, i)),
        ]
        + [anywhere] * wholes,
        out_shape=[
            jax.ShapeDtypeStruct((tokens, units), BF),
            jax.ShapeDtypeStruct((tokens, 2 * units), BF),
        ]
        + [whole] * wholes,
        scratch_shapes=[
            pltpu.VMEM((tokens, width), BF),
            pltpu.VMEM((tokens, width), BF),
            pltpu.SemaphoreType.DMA((2 * PIECES,)),
            pltpu.SemaphoreType.DMA((2,)),
        ],
        compiler_params=pltpu.CompilerParams(vmem_limit_bytes=48 * 2**20),
        cost_estimate=pl.CostEstimate(
            flops=2 * tokens * width * units * 3,
            bytes_accessed=4 * tokens * width * 2 + 6 * width * units + 6 * tokens * units,
            transcendentals=tokens * units,
        ),
    )(mat, mat, *normed, *tops)


def norm_inverse(values):
    return lax.rsqrt(jnp.mean(values * values, axis=-1, keepdims=True) + EPSILON)


def norm_back(grad, unit, inverse, gain):
    scaled = grad * gain
    return inverse * (scaled - unit * jnp.mean(scaled * unit, axis=-1, keepdims=True))


def wgrad(rows, columns):
    return lax.dot_general(rows, columns, COLS_C, preferred_element_type=F32).astype(BF)


def scaled_wgrad(rows, columns, gain):
    out = lax.dot_general(rows, columns, COLS_C, preferred_element_type=F32)
    return (out * gain[:, None]).astype(BF)


CHUNKS = ((0, 3),)


def layer_shards(
    hidden_in, out_grad, doc_lengths, norm_attn, query_gain, key_gain, query_weight, key_weight,
    value_weight, output_weight, norm_mlp, gate_weight, upward_weight, down_weight,
):
    d, z, y = lax.axis_index("dp"), lax.axis_index("blk"), lax.axis_index("fsdp")
    x_bit, c_bit, odd = d // 2, d % 2, z % 2
    coords = (x_bit, c_bit, y)
    width = hidden_in.shape[-1]
    docs = doc_lengths.shape[1]
    head = query_gain.shape[0] * 32
    groups = query_weight.shape[1] // key_weight.shape[1]
    total = hidden_in.shape[1] * 8
    hidden_units = gate_weight.shape[1]
    share = width // 32
    transposed = (((1,), (1,)), ((), ()))
    plain = (((1,), (0,)), ((), ()))

    sent = *send_rows(hidden_in, odd), *send_rows(out_grad, odd)
    small = jnp.concatenate(
        [v.astype(F32) for v in (norm_attn, norm_mlp, query_gain, key_gain)]
        + [after(doc_lengths, *sent).astype(F32).reshape(-1)]
    )
    tokens, top_own = rows_in(sent[:2], odd), rows_in(sent[2:], odd)
    small_all, small_last = small_gather(small, coords, z)

    pieces = jnp.concatenate(
        [w.reshape(share, 8, -1) for w in (after(query_weight, *sent), key_weight, value_weight)], axis=-1
    )
    pieces = jnp.transpose(pieces, (1, 0, 2)).reshape(2, 2, 2, share, -1)
    pieces = trade(pieces, x_bit, over_x, 0)
    pieces = trade(pieces, y, over_y, 2)
    qkv_own = trade(pieces, c_bit, over_c, 1)

    n_attn, n_head = norm_attn.shape[0], query_gain.shape[0]
    by_device = jnp.transpose(small_all, (1, 2, 0, 3, 4)).reshape(32, -1)
    by_blk = small_all.reshape(32, -1)
    gain_attn = by_blk[:, :n_attn].reshape(-1)
    gain_mlp = by_blk[:, n_attn : 2 * n_attn].reshape(-1)
    gain_query = by_device[:, 2 * n_attn : 2 * n_attn + n_head].reshape(-1)
    gain_key = by_device[:, 2 * n_attn + n_head : 2 * n_attn + 2 * n_head].reshape(-1)
    lengths = by_device[::8, 2 * n_attn + 2 * n_head :].astype(jnp.int32).reshape(4, 2, docs)
    ends_all = running_ends(lengths)
    ends = jnp.stack(
        [ends_all[(x_bit ^ dx) * 2 + z // 2, odd] for dx in range(2)]
    )
    place = jnp.arange(total, dtype=jnp.int32)
    start = jnp.zeros((2, total), jnp.int32)
    for doc in range(docs - 1):
        start = jnp.where(place[None] >= ends[:, doc : doc + 1], ends[:, doc : doc + 1], start)
    frequency = jnp.exp(
        jnp.arange(head // 2, dtype=F32) * (-2.0 / head) * math.log(ROPE_BASE)
    )
    angles = (place[None] - start).astype(F32)[..., None] * frequency
    cos_half, sine_half = jnp.cos(angles), jnp.sin(angles)
    cos_table = jnp.concatenate([cos_half, cos_half], axis=-1)
    sine_table = jnp.concatenate([-sine_half, sine_half], axis=-1)
    scalars = jnp.concatenate([jnp.stack([c_bit, y]), ends.reshape(-1)]).astype(jnp.int32)
    head_gains = jnp.concatenate(
        [gain_query[None], gain_key[None], jnp.zeros((6, head), F32)], axis=0
    )

    quarter = hidden_units // 4
    by_quarter = [w.reshape(-1, 4, quarter // UNIT_TILE, UNIT_TILE) for w in (gate_weight, upward_weight, down_weight)]
    weight_pieces = []
    for first, last in CHUNKS:
        gates, upwards, downs = (w[:, :, first:last] for w in by_quarter)
        piece = jnp.concatenate(
            [jnp.stack([gates, upwards], axis=3).reshape(*gates.shape[:2], -1), downs.reshape(*gates.shape[:2], -1)],
            axis=-1,
        )
        weight_pieces.append(jnp.transpose(piece, (1, 0, 2)).reshape(2, 2, piece.shape[0], -1))

    def layer_weights(piece, *before):
        half = over_x(after(pick(piece, 1 - x_bit, 0), *before))
        half = join(pick(piece, x_bit, 0), half, x_bit, 0)
        return trade(half, c_bit, over_c, 1).reshape(width // 4, -1)

    owns = [layer_weights(weight_pieces[0], qkv_own)]
    arrived = tokens
    tokens = [after(t, qkv_own, *top_own, *owns) for t in tokens]
    attn_own = jnp.concatenate([qkv_own.reshape(8 * share, -1), output_weight.reshape(4 * share, -1)])
    attn_all = blk_gather(after(attn_own, small_last, *arrived, *top_own)).reshape(4, 12 * share, -1)

    layer_in = [t.astype(F32) for t in tokens]
    inverse_attn = [norm_inverse(t) for t in layer_in]
    unit_attn = [t * i for t, i in zip(layer_in, inverse_attn, strict=True)]
    units1 = layer_gather(*[u.astype(BF) for u in unit_attn], (cos_table, sine_table))
    owns += [layer_weights(piece, units1[1], units1[3]) for piece in weight_pieces[1:]]
    mats = [blk_gather(after(own, *arrived, *top_own)) for own in owns]
    tops = layer_gather(*[after(t, units1[1], units1[3]) for t in top_own])
    qkv_mat = attn_all[:, : 8 * share].reshape(width, -1)
    scaled_mat = (qkv_mat.astype(F32) * gain_attn[:, None]).astype(BF)
    raw, units1_all = pieces_dot(units1, scaled_mat, plain, F32)
    out_all = after(attn_all, raw)[:, 8 * share :].reshape(2, 2, share, width)
    out_all = trade(out_all, y, over_y, 0)
    out_mat = sort_model(jnp.swapaxes(out_all, 0, 1).reshape(-1, width), BF)
    (mix,) = attend(scalars, raw, cos_table, sine_table, head_gains, groups, docs)
    mix = after(mix, tops[1], tops[3])
    mixed, _ = scatter_end(scatter_start(product_of(mix, out_mat, plain)))
    residual = [t + total_of(parts) for t, parts in zip(layer_in, mixed, strict=True)]
    inverse_mlp = [norm_inverse(t) for t in residual]
    unit_mlp = [t * i for t, i in zip(residual, inverse_mlp, strict=True)]
    normed2 = layer_gather(*[after((u * gain_mlp).astype(BF), *tops) for u in unit_mlp])

    hiddens, dboths, boths, downs, down_wgrads, both_wgrads = [], [], [], [], [], []
    dnormed2_part = mlp_part = None
    normed2_all = top_all = None
    for (first, last), mat in zip(CHUNKS, mats, strict=True):
        units = (last - first) * UNIT_TILE
        boths.append(mat[:, : 2 * units])
        downs.append(mat[:, 2 * units :])
        if normed2_all is None:
            hidden, dboth, normed2_all, top_all = units_pass(normed2, tops, mat)
        else:
            normed2_all = after(
                normed2_all, *down_wgrads, *both_wgrads, *(part[0] for part in dnormed2_part.values())
            )
            hidden, dboth = units_pass([normed2_all], [top_all], mat)
        hiddens.append(hidden)
        dboths.append(dboth)
        if last != CHUNKS[-1][1]:
            both_wgrads.append(wgrad(normed2_all, dboth))
            down_wgrads.append(wgrad(top_all, after(hidden, both_wgrads[-1])))
            part = product_of(after(dboth, down_wgrads[-1]), boths[-1], transposed, dnormed2_part)
            dnormed2_part = {1024: part(1024, 1536), 1536: part(1536, 2048), 0: part(0, 1024)}
    down_wgrads.append(wgrad(top_all, hiddens[-1]))
    state = scatter_start(
        product_of(after(dboths[-1], down_wgrads[-1]), boths[-1], transposed, dnormed2_part)
    )
    here, _, second, _ = state
    both_wgrads.append(wgrad(after(normed2_all, *second), dboths[-1]))
    dnormed2, third = scatter_end(state, both_wgrads[-1:])
    dnormed2 = [total_of(parts) for parts in dnormed2]

    gain_mlp_grad = sum(jnp.sum(g * u, axis=0) for g, u in zip(dnormed2, unit_mlp, strict=True))
    dresidual = [
        t.astype(F32) + norm_back(g, u, i, gain_mlp)
        for t, g, u, i in zip(top_own, dnormed2, unit_mlp, inverse_mlp, strict=True)
    ]
    both_last, down_last = both_wgrads[-1], down_wgrads[-1]
    both_wgrads = [blk_scatter(part) for part in both_wgrads]
    down_wgrads = [blk_scatter(part) for part in down_wgrads]
    spans = ((1024, 1536), (1536, 2048), (0, 1024))
    for hidden, down in zip(hiddens[:-1], downs[:-1], strict=True):
        part = product_of(after(hidden, *second), down, transposed, mlp_part)
        mlp_part = {first: part(first, last) for first, last in spans}
    mlp_product = product_of(after(hiddens[-1], *third), downs[-1], transposed, mlp_part)
    mlp_product = {first: mlp_product(first, last) for first, last in spans}
    dres = layer_gather(
        *[after(t.astype(BF), down_last) for t in dresidual],
        [both_last] + [part[0] for part in mlp_product.values()],
    )
    mlp_state = scatter_start(lambda first, *_: mlp_product[first], (dres[1], dres[3]))
    dmix, dres_all = pieces_dot(dres, out_mat, transposed, BF)
    out_wgrad = wgrad(mix, dres_all).reshape(2, 2, share, width)
    out_away = pick(out_wgrad, 1 - y, 1)
    dmix = after(dmix, out_away, *mlp_state[2], *both_wgrads[:-1], *down_wgrads[:-1])
    draw, dgains = attend(scalars, raw, cos_table, sine_table, head_gains, groups, docs, dmix)
    mlp_out, mlp_third = scatter_end(mlp_state, (draw,))
    draw = after(draw, *mlp_third)
    beside = {}

    def after_attention(sent):
        beside["qkv"] = scaled_wgrad(units1_all, after(draw, *sent), gain_attn)
        return beside["qkv"], *both_wgrads, *down_wgrads

    state = scatter_start(product_of(draw, qkv_mat, transposed), (), after_attention)
    second = state[2]
    dnormed1, third = scatter_end(state)
    dnormed1 = [total_of(parts) for parts in dnormed1]
    out_wgrad = join(pick(out_wgrad, y, 1), after(over_y(out_away), draw), y, 0).reshape(4 * share, width)
    attn_wgrad = jnp.concatenate(
        [beside["qkv"].reshape(4, 8 * share, -1), out_wgrad.reshape(4, 4 * share, -1)], axis=1
    )
    attn_wgrad = after(attn_wgrad.reshape(48 * share, -1), *both_wgrads, *down_wgrads)
    attn_wgrad = blk_scatter(attn_wgrad)
    qkv_wgrad, out_low = attn_wgrad[: 8 * share], attn_wgrad[8 * share :].reshape(share, width)
    out_wgrad = sort_model(out_low, F32)

    gain_attn_grad = sum(jnp.sum(g * u, axis=0) for g, u in zip(dnormed1, unit_attn, strict=True))
    input_grad = [
        (t + norm_back(g, u, i, gain_attn)).astype(BF)
        for t, g, u, i in zip(dresidual, dnormed1, unit_attn, inverse_attn, strict=True)
    ]
    layer_out = [
        after((t + total_of(parts)).astype(BF), *second)
        for t, parts in zip(residual, mlp_out, strict=True)
    ]
    layer_out = rows_out(*layer_out, odd)
    layer_out = keep_rows(after(layer_out[0], *input_grad), layer_out[1], odd, BF)
    sent = by_bit(odd, *input_grad), by_bit(odd, *input_grad[::-1])
    input_got = rows_back(sent)

    own = after(jnp.concatenate([*both_wgrads, *down_wgrads], axis=1), *second)
    own = own.reshape(2, 2, width // 16, -1)
    own = after(trade(own, c_bit, over_c, 1), attn_wgrad, *third)
    own_got = over_x(pick(own, 1 - x_bit, 0))
    swapped = join(pick(own, x_bit, 0), own_got, x_bit, 0).reshape(4, width // 16, -1)
    input_grad = keep_rows(after(input_got[0], own_got), input_got[1], odd, F32)
    gate_parts, upward_parts, down_parts = [], [], []
    for q in range(4):
        for tile in range(quarter // UNIT_TILE):
            cut = lambda i: swapped[q][:, i * UNIT_TILE : (i + 1) * UNIT_TILE]
            gate_parts.append(cut(2 * tile))
            upward_parts.append(cut(2 * tile + 1))
            down_parts.append(cut(2 * (quarter // UNIT_TILE) + tile))
    gate_wgrad, upward_wgrad, down_wgrad = (
        jnp.concatenate(parts, axis=1).astype(F32) for parts in (gate_parts, upward_parts, down_parts)
    )
    qkv_wgrad = qkv_wgrad.reshape(2, 2, 2, share, -1)
    qkv_wgrad = trade(trade(trade(qkv_wgrad, c_bit, over_c, 1), y, over_y, 2), x_bit, over_x, 0)
    qkv_wgrad = qkv_wgrad.reshape(8, share, -1)
    q_cols = groups * head
    query_wgrad = jnp.concatenate([qkv_wgrad[i][:, :q_cols] for i in range(8)], axis=1).astype(F32)
    key_wgrad = jnp.concatenate([qkv_wgrad[i][:, q_cols : q_cols + head] for i in range(8)], axis=1).astype(F32)
    value_wgrad = jnp.concatenate([qkv_wgrad[i][:, q_cols + head :] for i in range(8)], axis=1).astype(F32)

    dgains = jnp.sum(dgains, axis=0)
    small_grads = jnp.concatenate(
        [
            model_order(gain_attn_grad).reshape(32, -1),
            model_order(gain_mlp_grad).reshape(32, -1),
            dgains[0].reshape(32, -1),
            dgains[1].reshape(32, -1),
        ],
        axis=1,
    )
    small_grads = small_scatter(small_grads, coords, z, (own_got,))
    return (
        layer_out,
        input_grad,
        small_grads[:n_attn],
        small_grads[2 * n_attn : 2 * n_attn + n_head],
        small_grads[2 * n_attn + n_head :],
        query_wgrad,
        key_wgrad,
        value_wgrad,
        out_wgrad,
        small_grads[n_attn : 2 * n_attn],
        gate_wgrad,
        upward_wgrad,
        down_wgrad,
    )


def normalize(values, gain):
    inverse = lax.rsqrt(jnp.mean(values * values, axis=-1, keepdims=True) + EPSILON)
    return values * inverse * gain


def rotate(values, cos_table, sine_table):
    halfway = values.shape[-1] // 2
    turned = jnp.concatenate([-values[..., halfway:], values[..., :halfway]], axis=-1)
    return values * cos_table + turned * sine_table


def placement_of(lengths, offset, total):
    places = offset + jnp.arange(total, dtype=jnp.int32)
    ends = running_ends(lengths)
    before = (ends[:, None, :] <= places[None, :, None]).astype(jnp.int32)
    document = jnp.sum(before, axis=2)
    doc_start = jnp.sum(before * lengths[:, None, :], axis=2)
    return (document, places[None, :] - doc_start, places)


def rotary_tables(position, head_size):
    frequency = jnp.exp(
        jnp.arange(head_size // 2, dtype=jnp.float32) * (-2.0 / head_size) * math.log(ROPE_BASE)
    )
    angles = position.astype(jnp.float32)[..., None] * frequency
    angles = jnp.concatenate([angles, angles], axis=-1)
    return (jnp.cos(angles)[:, :, None, :], jnp.sin(angles)[:, :, None, :])


def head_path(raw_rows, gain, cos_table, sine_table):
    shaped = raw_rows.reshape(raw_rows.shape[0], raw_rows.shape[1], -1, gain.shape[0])
    return rotate(normalize(shaped, gain), cos_table, sine_table)


def block_size(total):
    return max((divisor for divisor in range(1, min(total, 512) + 1) if total % divisor == 0))


def silu_slope(gate_proj):
    logistic = jax.nn.sigmoid(gate_proj)
    return logistic * (1.0 + gate_proj * (1.0 - logistic))


def shards(
    hidden_in,
    out_grad,
    doc_lengths,
    norm_attn,
    query_gain,
    key_gain,
    query_weight,
    key_weight,
    value_weight,
    output_weight,
    norm_mlp,
    gate_weight,
    upward_weight,
    down_weight,
):
    attn_set = (
        lax.all_gather(query_weight, ("dp", "blk", "fsdp"), axis=0, tiled=True),
        lax.all_gather(key_weight, ("dp", "blk", "fsdp"), axis=0, tiled=True),
        lax.all_gather(value_weight, ("dp", "blk", "fsdp"), axis=0, tiled=True),
        lax.all_gather(output_weight, ("dp", "blk", "fsdp"), axis=0, tiled=True),
        lax.all_gather(norm_attn, ("dp", "blk", "fsdp"), axis=0, tiled=True),
        lax.all_gather(query_gain, ("dp", "blk", "fsdp"), axis=0, tiled=True),
        lax.all_gather(key_gain, ("dp", "blk", "fsdp"), axis=0, tiled=True),
        lax.all_gather(norm_mlp, ("dp", "blk", "fsdp"), axis=0, tiled=True),
    )
    query_mat, key_mat, value_mat, out_mat = (attn_set[0], attn_set[1], attn_set[2], attn_set[3])
    gain_attn = attn_set[4].astype(jnp.float32)
    gain_query = attn_set[5].astype(jnp.float32)
    gain_key = attn_set[6].astype(jnp.float32)
    gain_mlp = attn_set[7].astype(jnp.float32)
    gate_mat, upward_mat, down_mat = (
        lax.all_gather(gate_weight, ("dp", "blk"), axis=0, tiled=True),
        lax.all_gather(upward_weight, ("dp", "blk"), axis=0, tiled=True),
        lax.all_gather(down_weight, ("dp", "blk"), axis=0, tiled=True),
    )
    seq_count, local_rows, _width = hidden_in.shape
    head_size = gain_key.shape[0]
    heads_kv = key_mat.shape[1] // head_size
    heads_q = query_mat.shape[1] // head_size
    group_size = heads_q // heads_kv
    softmax_scale = 1.0 / math.sqrt(head_size)
    offset = lax.axis_index(("blk", "fsdp")) * local_rows
    query_doc, query_pos, query_place = placement_of(doc_lengths, offset, local_rows)
    cos_table, sine_table = rotary_tables(query_pos, head_size)
    layer_in = hidden_in.astype(jnp.float32)
    first_norm = normalize(layer_in, gain_attn).astype(jnp.bfloat16)
    query_raw = jnp.dot(first_norm, query_mat, preferred_element_type=jnp.float32)
    key_raw = jnp.dot(first_norm, key_mat, preferred_element_type=jnp.float32)
    value_rows = jnp.dot(first_norm, value_mat, preferred_element_type=jnp.float32).astype(
        jnp.bfloat16
    )
    query_rows = head_path(query_raw, gain_query, cos_table, sine_table).astype(jnp.bfloat16)
    query_rows = query_rows.reshape(seq_count, local_rows, heads_kv, group_size, head_size)
    key_rows = head_path(key_raw, gain_key, cos_table, sine_table).astype(jnp.bfloat16)
    key_rows = key_rows.reshape(seq_count, local_rows, heads_kv * head_size)

    def score_block(key_part, first_key):
        key_count = key_part.shape[1]
        key_heads = key_part.reshape(seq_count, key_count, heads_kv, head_size)
        scores = (
            jnp.einsum(
                "sckgd,spkd->skgcp", query_rows, key_heads, preferred_element_type=jnp.float32
            )
            * softmax_scale
        )
        key_doc, _key_pos, key_place = placement_of(doc_lengths, first_key, key_count)
        visible = (query_doc[:, None, None, :, None] == key_doc[:, None, None, None, :]) & (
            key_place[None, None, None, None, :] <= query_place[None, None, None, :, None]
        )
        return (scores, visible)

    def attend_block(running, key_part, value_part, first_key):
        run_max, run_total, run_sum = running
        scores, visible = score_block(key_part, first_key)
        masked = jnp.where(visible, scores, MASKED)
        new_max = jnp.maximum(run_max, jnp.max(masked, axis=-1))
        weights = jnp.where(visible, jnp.exp(masked - new_max[..., None]), 0.0)
        rescale = jnp.exp(run_max - new_max)
        value_heads = value_part.reshape(seq_count, -1, heads_kv, head_size)
        update = jnp.einsum(
            "skgcp,spkd->sckgd",
            weights.astype(jnp.bfloat16),
            value_heads,
            preferred_element_type=jnp.float32,
        )
        rescale_rows = jnp.transpose(rescale, (0, 3, 1, 2))[..., None]
        return (
            new_max,
            run_total * rescale + jnp.sum(weights, axis=-1),
            run_sum * rescale_rows + update,
        )

    start_carry = (
        jnp.full((seq_count, heads_kv, group_size, local_rows), MASKED, jnp.float32),
        jnp.zeros((seq_count, heads_kv, group_size, local_rows), jnp.float32),
        jnp.zeros((seq_count, local_rows, heads_kv, group_size, head_size), jnp.float32),
    )
    first_key = jnp.int32(0)
    key_part = lax.all_gather(key_rows, ("blk", "fsdp"), axis=1, tiled=True)
    value_part = lax.all_gather(value_rows, ("blk", "fsdp"), axis=1, tiled=True)
    piece_rows = key_part.shape[1]
    fold_block_len = block_size(piece_rows)

    def one_block(block_index, inner):
        begin_row = block_index * fold_block_len
        return attend_block(
            inner,
            lax.dynamic_slice_in_dim(key_part, begin_row, fold_block_len, 1),
            lax.dynamic_slice_in_dim(value_part, begin_row, fold_block_len, 1),
            first_key + begin_row,
        )

    running = lax.fori_loop(0, piece_rows // fold_block_len, one_block, start_carry)
    run_max, run_total, run_sum = running
    attn_mix = run_sum / jnp.transpose(run_total, (0, 3, 1, 2))[..., None]
    log_total = run_max + jnp.log(run_total)
    mix_rows = attn_mix.reshape(seq_count, local_rows, heads_q * head_size).astype(jnp.bfloat16)
    residual = layer_in + jnp.dot(mix_rows, out_mat, preferred_element_type=jnp.float32)
    second_norm = normalize(residual, gain_mlp).astype(jnp.bfloat16)
    pair_rows = lax.all_gather(second_norm, "fsdp", axis=1, tiled=True)
    gate_proj = jnp.dot(pair_rows, gate_mat, preferred_element_type=jnp.float32)
    upward_proj = jnp.dot(pair_rows, upward_mat, preferred_element_type=jnp.float32)
    hidden_rows = (jax.nn.silu(gate_proj) * upward_proj).astype(jnp.bfloat16)
    down_part = jnp.einsum("scf,df->scd", hidden_rows, down_mat, preferred_element_type=jnp.float32)
    mlp_out = lax.psum_scatter(
        down_part.astype(jnp.bfloat16), "fsdp", scatter_dimension=1, tiled=True
    ).astype(jnp.float32)
    layer_out = (residual + mlp_out).astype(jnp.bfloat16)
    top_grad = out_grad.astype(jnp.float32)
    gate_back, upward_back, down_back = (
        lax.all_gather(gate_weight, ("dp", "blk"), axis=0, tiled=True),
        lax.all_gather(upward_weight, ("dp", "blk"), axis=0, tiled=True),
        lax.all_gather(down_weight, ("dp", "blk"), axis=0, tiled=True),
    )
    pair_grad = lax.all_gather(out_grad, "fsdp", axis=1, tiled=True)
    hidden_grad = jnp.einsum(
        "scd,df->scf", pair_grad, down_back, preferred_element_type=jnp.float32
    )
    down_wgrad = jnp.einsum(
        "scd,scf->df", pair_grad, hidden_rows, preferred_element_type=jnp.float32
    )
    gate_grad = (hidden_grad * upward_proj * silu_slope(gate_proj)).astype(jnp.bfloat16)
    upward_grad = (hidden_grad * jax.nn.silu(gate_proj)).astype(jnp.bfloat16)
    gate_wgrad = jnp.einsum("scd,scf->df", pair_rows, gate_grad, preferred_element_type=jnp.float32)
    upward_wgrad = jnp.einsum(
        "scd,scf->df", pair_rows, upward_grad, preferred_element_type=jnp.float32
    )
    norm_part = jnp.einsum("scf,df->scd", gate_grad, gate_back, preferred_element_type=jnp.float32)
    norm_part = norm_part + jnp.einsum(
        "scf,df->scd", upward_grad, upward_back, preferred_element_type=jnp.float32
    )
    second_grad = lax.psum_scatter(
        norm_part.astype(jnp.bfloat16), "fsdp", scatter_dimension=1, tiled=True
    ).astype(jnp.float32)
    mlp_wgrads = (
        lax.psum_scatter(gate_wgrad, ("dp", "blk"), scatter_dimension=0, tiled=True),
        lax.psum_scatter(upward_wgrad, ("dp", "blk"), scatter_dimension=0, tiled=True),
        lax.psum_scatter(down_wgrad, ("dp", "blk"), scatter_dimension=0, tiled=True),
    )
    _second_value, second_pull = jax.vjp(normalize, residual, gain_mlp)
    residual_part, gain_mlp_grad = second_pull(second_grad)
    residual_grad = top_grad + residual_part
    query_back, key_back, value_back, out_back = (
        lax.all_gather(query_weight, ("dp", "blk", "fsdp"), axis=0, tiled=True),
        lax.all_gather(key_weight, ("dp", "blk", "fsdp"), axis=0, tiled=True),
        lax.all_gather(value_weight, ("dp", "blk", "fsdp"), axis=0, tiled=True),
        lax.all_gather(output_weight, ("dp", "blk", "fsdp"), axis=0, tiled=True),
    )
    residual_low = residual_grad.astype(jnp.bfloat16)
    out_wgrad = jnp.einsum(
        "sce,scd->ed", mix_rows, residual_low, preferred_element_type=jnp.float32
    )
    mix_grad = jnp.einsum("scd,ed->sce", residual_low, out_back, preferred_element_type=jnp.float32)
    mix_grad = mix_grad.astype(jnp.bfloat16).reshape(
        seq_count, local_rows, heads_kv, group_size, head_size
    )
    delta = jnp.transpose(jnp.sum(mix_grad.astype(jnp.float32) * attn_mix, axis=-1), (0, 2, 3, 1))
    key_all, value_all = (
        lax.all_gather(key_rows, ("blk", "fsdp"), axis=1, tiled=True),
        lax.all_gather(value_rows, ("blk", "fsdp"), axis=1, tiled=True),
    )
    full_rows = key_all.shape[1]
    block_len = block_size(full_rows)

    def back_block(block_index, running_back):
        query_acc, key_buffer, value_buffer = running_back
        first_key = block_index * block_len
        key_part = lax.dynamic_slice_in_dim(key_all, first_key, block_len, 1)
        value_part = lax.dynamic_slice_in_dim(value_all, first_key, block_len, 1)
        key_heads = key_part.reshape(seq_count, block_len, heads_kv, head_size)
        value_heads = value_part.reshape(seq_count, block_len, heads_kv, head_size)
        scores, visible = score_block(key_part, first_key)
        probs = jnp.where(
            visible, jnp.exp(jnp.where(visible, scores, MASKED) - log_total[..., None]), 0.0
        )
        probs_grad = jnp.einsum(
            "sckgd,spkd->skgcp", mix_grad, value_heads, preferred_element_type=jnp.float32
        )
        score_grad = (probs * (probs_grad - delta[..., None])).astype(jnp.bfloat16)
        query_acc = (
            query_acc
            + jnp.einsum(
                "skgcp,spkd->sckgd", score_grad, key_heads, preferred_element_type=jnp.float32
            )
            * softmax_scale
        )
        key_piece = (
            jnp.einsum(
                "skgcp,sckgd->spkd", score_grad, query_rows, preferred_element_type=jnp.float32
            )
            * softmax_scale
        )
        value_piece = jnp.einsum(
            "skgcp,sckgd->spkd",
            probs.astype(jnp.bfloat16),
            mix_grad,
            preferred_element_type=jnp.float32,
        )
        key_buffer = lax.dynamic_update_slice_in_dim(
            key_buffer, key_piece.reshape(seq_count, block_len, -1), first_key, 1
        )
        value_buffer = lax.dynamic_update_slice_in_dim(
            value_buffer, value_piece.reshape(seq_count, block_len, -1), first_key, 1
        )
        return (query_acc, key_buffer, value_buffer)

    back_init = (
        jnp.zeros((seq_count, local_rows, heads_kv, group_size, head_size), jnp.float32),
        jnp.zeros((seq_count, full_rows, heads_kv * head_size), jnp.float32),
        jnp.zeros((seq_count, full_rows, heads_kv * head_size), jnp.float32),
    )
    query_acc, key_buffer, value_buffer = lax.fori_loop(
        0, full_rows // block_len, back_block, back_init
    )
    key_grad, value_grad = (
        lax.psum_scatter(
            key_buffer.astype(jnp.bfloat16), ("blk", "fsdp"), scatter_dimension=1, tiled=True
        ).astype(jnp.float32),
        lax.psum_scatter(
            value_buffer.astype(jnp.bfloat16), ("blk", "fsdp"), scatter_dimension=1, tiled=True
        ).astype(jnp.float32),
    )

    def query_path(raw_rows, gain):
        return head_path(raw_rows, gain, cos_table, sine_table)

    _query_value, query_pull = jax.vjp(query_path, query_raw, gain_query)
    query_raw_grad, gain_query_grad = query_pull(
        query_acc.reshape(seq_count, local_rows, heads_q, head_size)
    )
    _key_value, key_pull = jax.vjp(query_path, key_raw, gain_key)
    key_raw_grad, gain_key_grad = key_pull(
        key_grad.reshape(seq_count, local_rows, heads_kv, head_size)
    )
    query_low = query_raw_grad.astype(jnp.bfloat16)
    key_low = key_raw_grad.astype(jnp.bfloat16)
    value_low = value_grad.astype(jnp.bfloat16)
    query_wgrad = jnp.einsum(
        "scd,sce->de", first_norm, query_low, preferred_element_type=jnp.float32
    )
    key_wgrad = jnp.einsum("scd,sce->de", first_norm, key_low, preferred_element_type=jnp.float32)
    value_wgrad = jnp.einsum(
        "scd,sce->de", first_norm, value_low, preferred_element_type=jnp.float32
    )
    first_grad = jnp.einsum(
        "sce,de->scd", query_low, query_back, preferred_element_type=jnp.float32
    )
    first_grad = first_grad + jnp.einsum(
        "sce,de->scd", key_low, key_back, preferred_element_type=jnp.float32
    )
    first_grad = first_grad + jnp.einsum(
        "sce,de->scd", value_low, value_back, preferred_element_type=jnp.float32
    )
    _first_value, first_pull = jax.vjp(normalize, layer_in, gain_attn)
    layer_part, gain_attn_grad = first_pull(first_grad)
    input_grad = residual_grad + layer_part
    attn_wgrads = (
        lax.psum_scatter(query_wgrad, ("dp", "blk", "fsdp"), scatter_dimension=0, tiled=True),
        lax.psum_scatter(key_wgrad, ("dp", "blk", "fsdp"), scatter_dimension=0, tiled=True),
        lax.psum_scatter(value_wgrad, ("dp", "blk", "fsdp"), scatter_dimension=0, tiled=True),
        lax.psum_scatter(out_wgrad, ("dp", "blk", "fsdp"), scatter_dimension=0, tiled=True),
        lax.psum_scatter(gain_attn_grad, ("dp", "blk", "fsdp"), scatter_dimension=0, tiled=True),
        lax.psum_scatter(gain_query_grad, ("dp", "blk", "fsdp"), scatter_dimension=0, tiled=True),
        lax.psum_scatter(gain_key_grad, ("dp", "blk", "fsdp"), scatter_dimension=0, tiled=True),
        lax.psum_scatter(gain_mlp_grad, ("dp", "blk", "fsdp"), scatter_dimension=0, tiled=True),
    )
    return (
        layer_out,
        input_grad,
        attn_wgrads[4],
        attn_wgrads[5],
        attn_wgrads[6],
        attn_wgrads[0],
        attn_wgrads[1],
        attn_wgrads[2],
        attn_wgrads[3],
        attn_wgrads[7],
        mlp_wgrads[0],
        mlp_wgrads[1],
        mlp_wgrads[2],
    )


def solution(mesh):
    sizes = dict(mesh.shape)
    layered = (sizes["dp"], sizes["blk"], sizes["fsdp"]) == (4, 4, 2)
    return jax.shard_map(
        layer_shards if layered else shards,
        mesh=mesh,
        in_specs=(
            P("dp", ("blk", "fsdp"), None),
            P("dp", ("blk", "fsdp"), None),
            P("dp", None),
            P(("dp", "blk", "fsdp")),
            P(("dp", "blk", "fsdp")),
            P(("dp", "blk", "fsdp")),
            P(("dp", "blk", "fsdp"), None),
            P(("dp", "blk", "fsdp"), None),
            P(("dp", "blk", "fsdp"), None),
            P(("dp", "blk", "fsdp"), None),
            P(("dp", "blk", "fsdp")),
            P(("dp", "blk"), "fsdp"),
            P(("dp", "blk"), "fsdp"),
            P(("dp", "blk"), "fsdp"),
        ),
        out_specs=(
            P("dp", ("blk", "fsdp"), None),
            P("dp", ("blk", "fsdp"), None),
            P(("dp", "blk", "fsdp")),
            P(("dp", "blk", "fsdp")),
            P(("dp", "blk", "fsdp")),
            P(("dp", "blk", "fsdp"), None),
            P(("dp", "blk", "fsdp"), None),
            P(("dp", "blk", "fsdp"), None),
            P(("dp", "blk", "fsdp"), None),
            P(("dp", "blk", "fsdp")),
            P(("dp", "blk"), "fsdp"),
            P(("dp", "blk"), "fsdp"),
            P(("dp", "blk"), "fsdp"),
        ),
        check_vma=False,
    )
```
